256 devices in a mesh: dp: 16 (over y, x_lo, core), mp: 16 (over z, x_hi).
Axes of the slice: x: 4 (x_hi: 2, x_lo: 2; x = x_hi * 2 + x_lo), y: 4, z: 8, core: 2. Of those that a mesh axis runs over, the one named last changes fastest.
Arguments:
- hidden: bfloat16 [32768, 7168], P('dp', 'mp'), may hold values from -32 to 32
- cotangent: bfloat16 [32768, 4096], P(('dp', 'mp')), may hold values from -128 to 128
- master: float32 [4096, 7168], P('dp', 'mp'), may hold values from -0.0625 to 0.0625
- moment_one: float32 [4096, 7168], P('dp', 'mp'), may hold values from -0.00048828125 to 0.00048828125
- moment_two: float32 [4096, 7168], P('dp', 'mp'), may hold values from 6.811959e-11 to 6.8119594e-09
Outputs:
- hidden_grad: bfloat16 [32768, 7168], P('dp', 'mp')
- new_weight: bfloat16 [4096, 7168], P(None, 'mp')
- new_master: float32 [4096, 7168], P('dp', 'mp')
- new_moment_one: float32 [4096, 7168], P('dp', 'mp')
- new_moment_two: float32 [4096, 7168], P('dp', 'mp')
The draws below stay inside these ranges and needn't reach their ends.
All inputs are finite; a program needn't handle non-finite values.
Results may differ from the reference program's by a relative error of at most 0.0049.
Values may be sent and summed in bfloat16 or wider, within the bound.
A program may use at most 128 MiB of HBM per device.

```python
import math
import jax
import jax.numpy as jnp
from jax import lax

D = 4096
FF = 7168
LEN = 2048
TOKENS = 32768


def shared_signs(key):
    first_sign = jax.random.rademacher(jax.random.fold_in(key, 11), (TOKENS, 1), dtype=jnp.float32)
    second_sign = jax.random.rademacher(jax.random.fold_in(key, 12), (TOKENS, 1), dtype=jnp.float32)
    return (first_sign, second_sign)


def rough_columns(key, breadth, spread):
    ramp_up = 2.0 ** (jnp.arange(breadth, dtype=jnp.float32) / (breadth - 1))
    return ramp_up * jnp.exp(jax.random.uniform(key, (breadth,), jnp.float32, -spread, spread))


def common_part(key, breadth, strength_one, strength_two, sign_pair):
    dir_one = jnp.clip(jax.random.normal(jax.random.fold_in(key, 21), (breadth,), jnp.float32), -4.0, 4.0)
    dir_two = jnp.clip(jax.random.normal(jax.random.fold_in(key, 22), (breadth,), jnp.float32), -4.0, 4.0)
    amp_one = (strength_one / TOKENS) ** 0.25
    amp_two = (strength_two / TOKENS) ** 0.25
    return amp_one * sign_pair[0] * dir_one[None, :] + amp_two * sign_pair[1] * dir_two[None, :]


def draw_hidden(key, part):
    sign_pair = shared_signs(key)
    key = jax.random.fold_in(key, 3)
    random_part = jnp.clip(jax.random.normal(jax.random.fold_in(key, 1), (TOKENS, FF), jnp.float32), -4.0, 4.0)
    spread = 0.4
    strength_one = 0.75
    strength_two = 0.75
    shared = common_part(jax.random.fold_in(key, 2), FF, strength_one, strength_two, sign_pair)
    column_scale = rough_columns(jax.random.fold_in(key, 4), FF, spread)
    return ((random_part + shared) * column_scale[None, :]).astype(jnp.bfloat16)


def draw_cotangent(key, part):
    sign_pair = shared_signs(key)
    key = jax.random.fold_in(key, 5)
    random_part = jnp.clip(jax.random.normal(jax.random.fold_in(key, 1), (TOKENS, D), jnp.float32), -4.0, 4.0)
    spread = 0.4
    strength_one = 0.75
    strength_two = 0.75
    shared = common_part(jax.random.fold_in(key, 2), D, strength_one, strength_two, sign_pair)
    column_scale = rough_columns(jax.random.fold_in(key, 4), D, spread)
    replicas = TOKENS // LEN
    pairing = jax.random.permutation(jax.random.fold_in(key, 6), replicas)
    replica_of_row = jnp.arange(TOKENS, dtype=jnp.int32) // LEN
    block_of_column = jnp.arange(D, dtype=jnp.int32) // (D // replicas)
    paired_block = pairing[replica_of_row]
    spike_factor = jnp.where(paired_block[:, None] == block_of_column[None, :], 4.0, 1.0)
    return ((random_part + shared) * column_scale[None, :] * spike_factor).astype(jnp.bfloat16)


def block_levels(rng, dims, split, smallest, top_value):
    def one(axis_at, parts):
        draws = jax.random.uniform(jax.random.fold_in(jax.random.fold_in(rng, 6), axis_at), (parts,), jnp.float32, smallest / len(split), top_value / len(split))
        return jnp.repeat(jnp.exp(draws), dims[axis_at] // parts).reshape((-1,) + (1,) * (len(dims) - axis_at - 1))

    loudness = one(*split[0])
    for cut in split[1:]:
        loudness = loudness * one(*cut)
    return loudness


def scatter_about(stream_key, shape, width, bound, cuts=(), kind=jnp.bfloat16):
    array = width * jax.random.normal(stream_key, shape, jnp.float32)
    if cuts:
        array = array * block_levels(stream_key, shape, cuts, -0.22, 0.18)
    return jnp.clip(array, -bound, bound).astype(kind)


def setup_inputs(seed: int = 0) -> dict:
    key_list = jax.random.split(jax.random.key(seed), 6)
    return {
        "hidden": draw_hidden(jax.random.fold_in(key_list[5], 71), 0),
        "cotangent": draw_cotangent(jax.random.fold_in(key_list[5], 71), 0),
        "master": scatter_about(key_list[2], (D, FF), FF ** -0.5, 0.0625, ((0, 16), (1, 16)), jnp.float32),
        "moment_one": scatter_about(key_list[3], (D, FF), (0.2 / (D * FF) ** 0.5), 0.00048828125, ((0, 16), (1, 16)), jnp.float32),
        "moment_two": jnp.clip(jnp.exp(math.log(6.811959440966575e-09) - 4.6051702 * jax.random.uniform(key_list[4], (D, FF), jnp.float32) ** block_levels(key_list[4], (D, FF), ((0, 16), (1, 16)), -0.2, 0.2)), 6.811959329944273e-11, 6.811959440966575e-09),
    }


def reference(hidden, cotangent, master, moment_one, moment_two):
    weight = master.astype(jnp.bfloat16)
    hidden_grad = jnp.dot(cotangent, weight, preferred_element_type=jnp.float32).astype(jnp.bfloat16)
    gradient = lax.dot_general(cotangent, hidden, (((0,), (0,)), ((), ())), preferred_element_type=jnp.float32)
    squares = jnp.sum(gradient * gradient)
    scale = jnp.minimum(1.0, 1.0 / (jnp.sqrt(squares) + 1e-06))
    clipped = scale * gradient
    new_moment_one = 0.9 * moment_one + 0.1 * clipped
    new_moment_two = 0.95 * moment_two + 0.05 * clipped * clipped
    first_hat = new_moment_one / (1.0 - 0.9 ** 10)
    second_hat = new_moment_two / (1.0 - 0.95 ** 10)
    new_master = master - 0.01 * (first_hat / (jnp.sqrt(second_hat) + 1e-08) + 0.1 * master)
    new_weight = new_master.astype(jnp.bfloat16)
    return (hidden_grad, new_weight, new_master, new_moment_one, new_moment_two)
```

```python
import functools

import jax
import jax.numpy as jnp
from jax import lax
from jax.experimental import pallas as pl
from jax.experimental.pallas import tpu as pltpu
from jax.sharding import PartitionSpec as P

F32 = jnp.float32
BF16 = jnp.bfloat16
NT = (((1,), (1,)), ((), ()))
MESH = pl.DeviceIdType.MESH
FC = 448
NK = 8


def rem(a, n):
    return lax.rem(a, jnp.int32(n))


def div(a, n):
    return lax.div(a, jnp.int32(n))


def kernel(
    hid, cot, mas, m1, m2,
    hg_out, nw_out, nm_out, n1_out, n2_out,
    cbuf, wbuf, hbuf, ht, hts, hrel, gs, gr,
    yfs, yfr, yns, ynr, xs, xr, ga, acc, hgs, hgrel,
    masb, m1b, m2b, nwv, ns, nr,
    lsem, csem, zs, zr, hss, hsr, wxs, wxr, wys, wyr, wds, wdr,
    ds_, dr, yf_s, yf_r, yn_s, yn_r, x_s, x_r, g_s, g_r, n_s, n_r, o_s, o_r,
):
    dp = lax.axis_index("dp")
    mp = lax.axis_index("mp")
    core = rem(dp, 2)
    xlo = rem(div(dp, 2), 2)
    y = div(dp, 4)
    h = rem(mp, 2)
    z = div(mp, 2)
    x = h * 2 + xlo
    xr1, xl1, x2 = rem(x + 1, 4), rem(x + 3, 4), rem(x + 2, 4)
    yr1, yl1, y2 = rem(y + 1, 4), rem(y + 3, 4), rem(y + 2, 4)

    def dev(xx=x, yy=y, zz=z, cc=core):
        return ((yy * 2 + rem(xx, 2)) * 2 + cc, zz * 2 + div(xx, 2))

    def rc(src, dst, ss, rs, to):
        return pltpu.make_async_remote_copy(
            src_ref=src, dst_ref=dst, send_sem=ss, recv_sem=rs, device_id=to, device_id_type=MESH
        )

    me = dev(cc=1 - core)
    sib = dev(cc=1 - core)

    loads = [
        pltpu.make_async_copy(mas, masb, lsem.at[0]),
        pltpu.make_async_copy(hid, hbuf, lsem.at[1]),
        pltpu.make_async_copy(m1, m1b, lsem.at[2]),
        pltpu.make_async_copy(m2, m2b, lsem.at[3]),
    ]
    zrow = pl.multiple_of(z * 128, 128)
    for k in range(NK):
        q, p = k // 2, 1 - k % 2
        r, half = q // 2, q % 2
        xl_ = 1 - xlo if r else xlo
        c_ = 1 - core if p else core
        for yy in range(4):
            off = pl.multiple_of(((yy * 2 + xl_) * 2 + c_) * 256 + half * 128, 128)
            pltpu.make_async_copy(
                cot.at[:, pl.ds(off, 128)],
                cbuf.at[k, pl.ds(zrow, 128), pl.ds(yy * 128, 128)],
                csem.at[k],
            ).start()
        if k == 0:
            loads[0].start()
            loads[1].start()
    loads[2].start()
    loads[3].start()

    barrier = pltpu.get_barrier_semaphore()
    peers = [sib]
    for xx in (xr1, xl1, x2):
        peers += [dev(xx=xx), dev(xx=xx, cc=1 - core)]
    peers += [dev(yy=yy) for yy in (yr1, yl1, y2)]
    peers += [dev(zz=rem(z + i, 8)) for i in range(1, 8)]
    for to in peers:
        pl.semaphore_signal(barrier, inc=1, device_id=to, device_id_type=MESH)
    pl.semaphore_wait(barrier, len(peers))

    zto = (dev(zz=rem(z + 1, 8)), dev(zz=rem(z + 7, 8)))

    def zcopy(d, k, hop, sending):
        if d == 0:
            slot = rem(z + 16 - hop - (0 if sending else 1), 8)
        else:
            slot = rem(z + hop + (0 if sending else 1), 8)
        row, n = slot * 128, 128
        if hop == 3:
            n = 64
            row = row + 64 * d
        ref = cbuf.at[k, pl.ds(pl.multiple_of(row, 64), n), :]
        return rc(ref, ref, zs.at[d, k, hop], zr.at[d, k, hop], zto[d])

    def zring(s):
        for hop in (3, 2, 1, 0):
            k = s - hop

            @pl.when((k >= 0) & (k < NK))
            def _(hop=hop, k=k):
                if hop == 0:
                    own = cbuf.at[k, pl.ds(zrow, 128), :]
                    pltpu.make_async_copy(own, own, csem.at[k]).wait()
                for d in (0, 1):
                    if hop > 0:
                        zcopy(d, k, hop - 1, False).wait_recv()
                    zcopy(d, k, hop, True).start()

    eye = (
        lax.broadcasted_iota(jnp.int32, (FC, FC), 0) == lax.broadcasted_iota(jnp.int32, (FC, FC), 1)
    ).astype(BF16)

    def wblk(xx, yy, p, rows=None):
        lanes = pl.ds(pl.multiple_of(yy * 128, 128), 128)
        r_ = slice(None) if rows is None else pl.ds(rows[0], rows[1])
        return wbuf.at[rem(xx, 2), :, p, div(xx, 2), r_, lanes]

    def wx(d, far, sending):
        to = dev(xx=xr1 if d == 0 else xl1)
        if not far:
            src = x if sending else (xl1 if d == 0 else xr1)
            blk = wblk(src, y, 0)
        else:
            src = (xl1 if d == 0 else xr1) if sending else x2
            blk = wblk(src, y, 0, (d * 224, 224))
        i = 2 * far + d
        return rc(blk, blk, wxs.at[i], wxr.at[i], to)

    def wy(j, d, far, sending):
        xx = rem(x + j, 4)
        to = dev(yy=yr1 if d == 0 else yl1)
        if not far:
            src = y if sending else (yl1 if d == 0 else yr1)
            blk = wblk(xx, src, 0)
        else:
            src = (yl1 if d == 0 else yr1) if sending else y2
            blk = wblk(xx, src, 0, (d * 224, 224))
        i = 2 * far + d
        return rc(blk, blk, wys.at[j, i], wyr.at[j, i], to)

    def wd(j):
        xx = rem(x + j, 4)
        src = wbuf.at[rem(xx, 2), :, 0, div(xx, 2), :, :]
        dst = wbuf.at[rem(xx, 2), :, 1, div(xx, 2), :, :]
        return rc(src, dst, wds.at[j], wdr.at[j], sib)

    def hsend(d):
        src = hts.at[pl.ds(d * 224, 224), :]
        return rc(src, hrel.at[d], hss.at[d], hsr.at[d], dev(xx=xr1 if d == 0 else xl1))

    def hforward(d):
        to = dev(xx=xr1 if d == 0 else xl1)
        f_src = div(xl1 if d == 0 else xr1, 2)
        dst = ht.at[f_src, pl.ds(d * 224, 224), :]
        return rc(hrel.at[d], dst, hss.at[2 + d], hsr.at[2 + d], to)

    def hwait(d):
        dst = ht.at[1 - h, pl.ds(d * 224, 224), :]
        rc(dst, dst, hss.at[2 + d], hsr.at[2 + d], sib).wait_recv()

    def gd(q, f):
        return rc(gs.at[q, f], gr.at[q, f], ds_.at[q, f], dr.at[q, f], sib)

    def gyfar(q, f):
        return rc(
            yfs.at[q, f], yfr.at[q, f], yf_s.at[q, f], yf_r.at[q, f], dev(yy=yr1 if f == 0 else yl1)
        )

    def gynear(q, d):
        return rc(
            yns.at[q, d], ynr.at[q, d], yn_s.at[q, d], yn_r.at[q, d], dev(yy=yr1 if d == 0 else yl1)
        )

    def lanes(yy):
        return pl.ds(pl.multiple_of(yy * 128, 128), 128)

    def gradient_chunk(kc):
        q = div(kc, 2)
        part = kc - 2 * q
        for d in (0, 1):
            zcopy(d, kc, 3, False).wait_recv()

        @pl.when(part == 0)
        def _():
            def body(f, c):
                gs[q, f] = jnp.dot(ht[f], cbuf[kc], preferred_element_type=F32)
                gd(q, f).start()
                return c

            lax.fori_loop(0, 2, body, 0)

        @pl.when(part == 1)
        def _():
            def body(f, c):
                gd(q, f).wait_recv()
                gr[q, f] = gr[q, f] + jnp.dot(ht[f], cbuf[kc], preferred_element_type=F32)
                yfs[q, f] = gr[q, f, :, lanes(y2)].astype(BF16)
                return c

            lax.fori_loop(0, 2, body, 0)
            for f in (0, 1):
                gyfar(q, f).start()

    def ystep2(q):
        for f in (0, 1):
            gyfar(q, f).wait_recv()
        yns[q, 0, 0] = (gr[q, 0, :, lanes(yr1)] + yfr[q, 0].astype(F32)).astype(BF16)
        yns[q, 0, 1] = gr[q, 1, :, lanes(yr1)].astype(BF16)
        gynear(q, 0).start()
        yns[q, 1, 0] = gr[q, 0, :, lanes(yl1)].astype(BF16)
        yns[q, 1, 1] = (gr[q, 1, :, lanes(yl1)] + yfr[q, 1].astype(F32)).astype(BF16)
        gynear(q, 1).start()

    def xsend(q, i, sending):
        half = q % 2
        if q < 2:
            return rc(xs.at[q, 0], xr.at[half, 2], x_s.at[q, 0], x_r.at[half, 2], dev(xx=x2))
        if sending:
            return rc(
                xs.at[q, i], xr.at[half, h], x_s.at[q, i], x_r.at[half, h], dev(xx=i * 2 + 1 - xlo)
            )
        return rc(xs.at[q, i], xr.at[half, i], x_s.at[q, i], x_r.at[half, i], dev(xx=x2))

    def ystep3(q):
        for d in (0, 1):
            gynear(q, d).wait_recv()

        def total(f):
            return (
                gr[q, f, :, lanes(y)] + ynr[q, 0, f].astype(F32) + ynr[q, 1, f].astype(F32)
            )

        if q < 2:
            ga[q] = total(h)
            xs[q, 0] = total(1 - h).astype(BF16)
            xsend(q, 0, True).start()
        else:
            for f in (0, 1):
                xs[q, f] = total(f).astype(BF16)
                xsend(q, f, True).start()

    def wchunk(u, p, f):
        r, half = div(u, 2), rem(u, 2)
        xl_ = xlo + r - 2 * xlo * r
        return wbuf[xl_, half, p, f]

    def hg_pair(u):
        def body(i, c):
            f, t = div(i, 4), rem(i, 4)
            rows = pl.ds(pl.multiple_of(t * 256, 256), 256)
            a = lax.dot_general(cbuf[2 * u, rows, :], wchunk(u, 1, f), NT, preferred_element_type=F32)
            a += lax.dot_general(
                cbuf[2 * u + 1, rows, :], wchunk(u, 0, f), NT, preferred_element_type=F32
            )

            @pl.when(u == 0)
            def _():
                acc[f, rows, :] = a

            @pl.when((u > 0) & (u < 3))
            def _():
                acc[f, rows, :] = acc[f, rows, :] + a

            @pl.when(u == 3)
            def _():
                out = (acc[f, rows, :] + a).astype(BF16)
                hgs[f, pl.ds(2 * t, 2)] = out.reshape(2, 128, FC)

            return c

        lax.fori_loop(0, 8, body, 0)

    def hgsend(d):
        src = hgs.at[1 - h, pl.ds(4 * d, 4)]
        return rc(src, hgrel.at[d], g_s.at[d], g_r.at[d], dev(xx=xr1 if d == 0 else xl1))

    def hgforward(d):
        to = dev(xx=xr1 if d == 0 else xl1)
        par = div(xl1 if d == 0 else xr1, 2)
        return rc(hgrel.at[d], hg_out.at[pl.ds(4 * d, 4), par], g_s.at[2 + d], g_r.at[2 + d], to)

    def hgwait(d):
        dst = hg_out.at[pl.ds(4 * d, 4), 1 - h]
        rc(dst, dst, g_s.at[2 + d], g_r.at[2 + d], sib).wait_recv()

    zring(jnp.int32(0))
    loads[0].wait()
    wt = lax.dot_general(eye, masb[...].astype(BF16), NT, preferred_element_type=F32).astype(BF16)
    for half in (0, 1):
        wbuf[xlo, half, 0, h, :, lanes(y)] = wt[:, half * 128 : half * 128 + 128]
    wx(0, 0, True).start()
    wx(1, 0, True).start()
    wy(0, 0, 0, True).start()
    wy(0, 1, 0, True).start()
    loads[1].wait()

    def transpose_hidden(par, dst):
        for t in range(4):
            b = hbuf[pl.ds(2 * t, 2), par].reshape(256, FC)
            dst[:, t * 256 : t * 256 + 256] = lax.dot_general(
                eye, b, NT, preferred_element_type=F32
            ).astype(BF16)

    transpose_hidden(1 - h, hts)
    for d in (0, 1):
        hsend(d).start()
    transpose_hidden(h, ht.at[h])

    def tick(s, c):
        zring(s)

        @pl.when(s == 1)
        def _():
            for d in (0, 1):
                wx(d, 0, False).wait_recv()
            for d in (0, 1):
                wx(d, 1, True).start()
            for j in (1, 3):
                for d in (0, 1):
                    wy(j, d, 0, True).start()

        @pl.when(s == 2)
        def _():
            for d in (0, 1):
                wx(d, 1, False).wait_recv()
            for d in (0, 1):
                wy(2, d, 0, True).start()

        @pl.when(s == 3)
        def _():
            for d in (0, 1):
                hsend(d).wait_recv()
                hforward(d).start()

        @pl.when(s == 4)
        def _():
            for d in (0, 1):
                hwait(d)

        @pl.when(s == 5)
        def _():
            for j in range(4):
                for d in (0, 1):
                    wy(j, d, 0, False).wait_recv()
                    wy(j, d, 1, True).start()

        @pl.when(s == 7)
        def _():
            for j in range(4):
                for d in (0, 1):
                    wy(j, d, 1, False).wait_recv()
                wd(j).start()

        for q in range(3):

            @pl.when(s == 6 + 2 * q)
            def _(q=q):
                ystep2(q)

            @pl.when(s == 7 + 2 * q)
            def _(q=q):
                ystep3(q)

        @pl.when(s >= 4)
        def _():
            gradient_chunk(s - 4)

        @pl.when(s == 8)
        def _():
            for j in range(4):
                wd(j).wait_recv()

        @pl.when(s >= 8)
        def _():
            hg_pair(s - 8)

        return c

    lax.fori_loop(1, 12, tick, 0)

    for d in (0, 1):
        hgsend(d).start()
    own_hg = pltpu.make_async_copy(hgs.at[h], hg_out.at[:, h], lsem.at[4])
    own_hg.start()
    ystep2(3)
    ystep3(3)
    for d in (0, 1):
        hgsend(d).wait_recv()
        hgforward(d).start()
    loads[2].wait()
    loads[3].wait()
    sq = jnp.zeros((8, 128), F32)
    gt = []
    for half in (0, 1):
        xsend(half, 0, False).wait_recv()
        for i in (0, 1):
            xsend(2 + half, i, False).wait_recv()
        g = (
            ga[half]
            + xr[half, 2].astype(F32)
            + xr[half, 0].astype(F32)
            + xr[half, 1].astype(F32)
        )
        ga[half] = g
        sq = sq + jnp.sum((g * g).reshape(FC // 8, 8, 128), axis=0)

    groups = [
        [dev(cc=1 - core)]
        + [dev(xx=rem(x + i, 4), cc=c_) for i in (1, 2, 3) for c_ in (core, 1 - core)],
        [dev(yy=rem(y + i, 4)) for i in (1, 2, 3)],
        [dev(zz=rem(z + i, 8)) for i in range(1, 8)],
    ]
    sends = []
    for ph, group in enumerate(groups):
        ns[ph] = sq
        cps = [
            rc(ns.at[ph], nr.at[ph, i], n_s.at[ph, i], n_r.at[ph, i], to)
            for i, to in enumerate(group)
        ]
        for cp in cps:
            cp.start()
        sends += cps
        for i, cp in enumerate(cps):
            cp.wait_recv()
            sq = sq + nr[ph, i]
    squares = jnp.sum(sq, keepdims=True)
    scale = jnp.minimum(1.0, 1.0 / (jnp.sqrt(squares) + 1e-06))

    for half in (0, 1):
        rows = pl.ds(half * 128, 128)
        clipped = scale * jnp.transpose(ga[half])
        nm1 = 0.9 * m1b[rows, :] + 0.1 * clipped
        nm2 = 0.95 * m2b[rows, :] + 0.05 * clipped * clipped
        first_hat = nm1 / (1.0 - 0.9**10)
        second_hat = nm2 / (1.0 - 0.95**10)
        w = masb[rows, :]
        nmas = w - 0.01 * (first_hat / (jnp.sqrt(second_hat) + 1e-08) + 0.1 * w)
        m1b[rows, :] = nm1
        m2b[rows, :] = nm2
        masb[rows, :] = nmas
        nwv[rows, :] = nmas.astype(BF16)

    def nblk(yy, j, half=None, cc=core):
        xl_ = 1 - xlo if j else xlo
        off = ((yy * 2 + xl_) * 2 + cc) * 256
        if half is None:
            return nw_out.at[pl.ds(pl.multiple_of(off, 256), 256), :]
        return nw_out.at[pl.ds(pl.multiple_of(off + half * 128, 128), 128), :]

    def cp(src, dst, i, to):
        return rc(src, dst, o_s.at[i], o_r.at[i], to)

    to_y = (dev(yy=yr1), dev(yy=yl1))
    from_y = (yl1, yr1)
    to_x = dev(xx=h * 2 + 1 - xlo)
    outs = []

    def go(c):
        c.start()
        outs.append(c)

    def await_(blk, i):
        cp(blk, blk, i, sib).wait_recv()

    go(cp(nwv, nblk(y, 0), 8, to_x))
    for d in (0, 1):
        go(cp(nwv, nblk(y, 0), d, to_y[d]))
    go(cp(nwv, nblk(y, 0), 9, sib))
    finals = [
        pltpu.make_async_copy(nwv, nblk(y, 0), lsem.at[0]),
        pltpu.make_async_copy(masb, nm_out, lsem.at[1]),
        pltpu.make_async_copy(m1b, n1_out, lsem.at[2]),
        pltpu.make_async_copy(m2b, n2_out, lsem.at[3]),
    ]
    for c in finals:
        c.start()
    b = nblk(y, 1)
    await_(b, 8)
    for d in (0, 1):
        go(cp(b, b, 2 + d, to_y[d]))
    go(cp(b, b, 10, sib))
    for j in (0, 1):
        for d in (0, 1):
            b = nblk(from_y[d], j)
            await_(b, 2 * j + d)
            half = nblk(from_y[d], j, d)
            go(cp(half, half, 4 + 2 * j + d, to_y[d]))
            go(cp(b, b, 11 + 2 * j + d, sib))
    for j in (0, 1):
        for d in (0, 1):
            await_(nblk(y2, j, d), 4 + 2 * j + d)
        b = nblk(y2, j)
        go(cp(b, b, 15 + j, sib))
    oc = 1 - core
    await_(nblk(y, 0, cc=oc), 9)
    await_(nblk(y, 1, cc=oc), 10)
    for j in (0, 1):
        for d in (0, 1):
            await_(nblk(from_y[d], j, cc=oc), 11 + 2 * j + d)
        await_(nblk(y2, j, cc=oc), 15 + j)

    for d in (0, 1):
        hgwait(d)
    own_hg.wait()
    for c in finals:
        c.wait()
    for c in outs + sends:
        c.wait_send()
    for d in (0, 1):
        hgsend(d).wait_send()
        hgforward(d).wait_send()
        hsend(d).wait_send()
        hforward(d).wait_send()
        for far in (0, 1):
            wx(d, far, True).wait_send()
            for j in range(4):
                wy(j, d, far, True).wait_send()
    for j in range(4):
        wd(j).wait_send()
    for q in range(4):
        for f in (0, 1):
            gd(q, f).wait_send()
            gyfar(q, f).wait_send()
            gynear(q, f).wait_send()
            if q >= 2 or f == 0:
                xsend(q, f, True).wait_send()

    def drain(k, c):
        for hop in range(4):
            for d in (0, 1):
                zcopy(d, k, hop, True).wait_send()
        return c

    lax.fori_loop(0, NK, drain, 0)


def local(hidden, cotangent, master, moment_one, moment_two):
    dma = pltpu.SemaphoreType.DMA
    any_ = pl.BlockSpec(memory_space=pl.ANY)
    v = pltpu.VMEM
    scratch = [
        v((NK, 1024, 512), BF16),
        v((2, 2, 2, 2, FC, 512), BF16),
        v((8, 2, 128, FC), BF16),
        v((2, FC, 1024), BF16),
        v((FC, 1024), BF16),
        v((2, 224, 1024), BF16),
        v((4, 2, FC, 512), F32),
        v((4, 2, FC, 512), F32),
        v((4, 2, FC, 128), BF16),
        v((4, 2, FC, 128), BF16),
        v((4, 2, 2, FC, 128), BF16),
        v((4, 2, 2, FC, 128), BF16),
        v((4, 2, FC, 128), BF16),
        v((2, 3, FC, 128), BF16),
        v((2, FC, 128), F32),
        v((2, 1024, FC), F32),
        v((2, 8, 128, FC), BF16),
        v((2, 4, 128, FC), BF16),
        v((256, FC), F32),
        v((256, FC), F32),
        v((256, FC), F32),
        v((256, FC), BF16),
        v((3, 8, 128), F32),
        v((3, 7, 8, 128), F32),
        dma((5,)),
        dma((NK,)),
        dma((2, NK, 4)), dma((2, NK, 4)),
        dma((4,)), dma((4,)),
        dma((4,)), dma((4,)),
        dma((4, 4)), dma((4, 4)),
        dma((4,)), dma((4,)),
        dma((4, 2)), dma((4, 2)),
        dma((4, 2)), dma((4, 2)),
        dma((4, 2)), dma((4, 2)),
        dma((4, 2)), dma((2, 3)),
        dma((4,)), dma((4,)),
        dma((3, 7)), dma((3, 7)),
        dma((17,)), dma((17,)),
    ]
    sds = jax.ShapeDtypeStruct
    hg, nw, nm, n1, n2 = pl.pallas_call(
        kernel,
        out_shape=(
            sds((8, 2, 128, FC), BF16),
            sds((4096, FC), BF16),
            sds((256, FC), F32),
            sds((256, FC), F32),
            sds((256, FC), F32),
        ),
        in_specs=[any_] * 5,
        out_specs=(any_,) * 5,
        scratch_shapes=scratch,
        compiler_params=pltpu.CompilerParams(
            collective_id=0, has_side_effects=True, vmem_limit_bytes=63 * 2**20
        ),
        cost_estimate=pl.CostEstimate(
            flops=15_032_385_536, bytes_accessed=16_000_000, transcendentals=0
        ),
        name="fused_backward",
    )(hidden.reshape(8, 2, 128, FC), cotangent, master, moment_one, moment_two)
    return (hg.reshape(2048, FC), nw, nm, n1, n2)


def solution(mesh):
    return jax.shard_map(
        local,
        mesh=mesh,
        in_specs=(
            P("dp", "mp"),
            P(("dp", "mp"), None),
            P("dp", "mp"),
            P("dp", "mp"),
            P("dp", "mp"),
        ),
        out_specs=(P("dp", "mp"), P(None, "mp"), P("dp", "mp"), P("dp", "mp"), P("dp", "mp")),
        check_vma=False,
    )
```

```python
import functools

import jax
import jax.numpy as jnp
from jax import lax
from jax.experimental import pallas as pl
from jax.experimental.pallas import tpu as pltpu
from jax.sharding import PartitionSpec as P

F32 = jnp.float32
BF16 = jnp.bfloat16
NT = (((1,), (1,)), ((), ()))
MESH = pl.DeviceIdType.MESH
FC = 448
NK = 8


def rem(a, n):
    return lax.rem(a, jnp.int32(n))


def div(a, n):
    return lax.div(a, jnp.int32(n))


def kernel(
    hid, cot, mas, m1, m2,
    hg_out, nw_out, nm_out, n1_out, n2_out,
    cbuf, wbuf, ht, hts, gs, gr,
    yfs, yfr, yns, ynr, xs, xr, ga, acc, hgs,
    masb, m1b, m2b, nwb, ns, nr,
    lsem, csem, zs, zr, hss, hsr, wxs, wxr, wys, wyr, wds, wdr,
    ds_, dr, yf_s, yf_r, yn_s, yn_r, x_s, x_r, g_s, g_r, n_s, n_r, o_s, o_r, w_s,
):
    dp = lax.axis_index("dp")
    mp = lax.axis_index("mp")
    core = rem(dp, 2)
    xlo = rem(div(dp, 2), 2)
    y = div(dp, 4)
    h = rem(mp, 2)
    z = div(mp, 2)
    x = h * 2 + xlo
    xr1, xl1, x2 = rem(x + 1, 4), rem(x + 3, 4), rem(x + 2, 4)
    yr1, yl1, y2 = rem(y + 1, 4), rem(y + 3, 4), rem(y + 2, 4)

    def dev(xx=x, yy=y, zz=z, cc=core):
        return ((yy * 2 + rem(xx, 2)) * 2 + cc, zz * 2 + div(xx, 2))

    def rc(src, dst, ss, rs, to):
        return pltpu.make_async_remote_copy(
            src_ref=src, dst_ref=dst, send_sem=ss, recv_sem=rs, device_id=to, device_id_type=MESH
        )

    sib = dev(cc=1 - core)

    loads = [
        pltpu.make_async_copy(mas, masb, lsem.at[0]),
        pltpu.make_async_copy(m1, m1b, lsem.at[1]),
        pltpu.make_async_copy(m2, m2b, lsem.at[2]),
    ]
    zrow = pl.multiple_of(z * 128, 128)
    for k in range(NK):
        q, p = k // 2, 1 - k % 2
        r, half = q // 2, q % 2
        xl_ = 1 - xlo if r else xlo
        c_ = 1 - core if p else core
        for yy in range(4):
            off = pl.multiple_of(((yy * 2 + xl_) * 2 + c_) * 256 + half * 128, 128)
            pltpu.make_async_copy(
                cot.at[:, pl.ds(off, 128)],
                cbuf.at[k, pl.ds(zrow, 128), pl.ds(yy * 128, 128)],
                csem.at[k],
            ).start()
        if k == 0:
            loads[0].start()
            for par, sem in ((1 - h, 3), (h, 4)):
                for t in range(8):
                    src = hid.at[:, pl.ds(pl.multiple_of((2 * t + par) * 128, 128), 128)]
                    dst = hts if sem == 3 else ht.at[h]
                    dst = dst.at[:, pl.ds(t * 128, 128)]
                    pltpu.make_async_copy(src, dst, lsem.at[sem]).start()
    loads[1].start()
    loads[2].start()

    barrier = pltpu.get_barrier_semaphore()
    peers = [sib]
    for xx in (xr1, xl1, x2):
        peers += [dev(xx=xx), dev(xx=xx, cc=1 - core)]
    peers += [dev(yy=yy) for yy in (yr1, yl1, y2)]
    peers += [dev(zz=rem(z + i, 8)) for i in range(1, 8)]
    for to in peers:
        pl.semaphore_signal(barrier, inc=1, device_id=to, device_id_type=MESH)
    pl.semaphore_wait(barrier, len(peers))

    zto = (dev(zz=rem(z + 1, 8)), dev(zz=rem(z + 7, 8)))

    def zcopy(d, k, hop, sending):
        if d == 0:
            slot = rem(z + 16 - hop - (0 if sending else 1), 8)
        else:
            slot = rem(z + hop + (0 if sending else 1), 8)
        row, n = slot * 128, 128
        if hop == 3:
            n = 64
            row = row + 64 * d
        ref = cbuf.at[k, pl.ds(pl.multiple_of(row, 64), n), :]
        return rc(ref, ref, zs.at[d, k, hop], zr.at[d, k, hop], zto[d])

    def zown(k):
        own = cbuf.at[k, pl.ds(zrow, 128), :]
        pltpu.make_async_copy(own, own, csem.at[k]).wait()
        for d in (0, 1):
            zcopy(d, k, 0, True).start()

    def zring(s):
        for hop in (3, 2, 1):
            k = s - hop

            @pl.when((k >= 0) & (k < NK))
            def _(hop=hop, k=k):
                for d in (0, 1):
                    zcopy(d, k, hop - 1, False).wait_recv()
                    zcopy(d, k, hop, True).start()

        @pl.when(s < NK - 1)
        def _():
            zown(s + 1)

    def wblk(xx, yy, p, rows=None):
        lanes = pl.ds(pl.multiple_of(yy * 128, 128), 128)
        r_ = slice(None) if rows is None else pl.ds(rows[0], rows[1])
        return wbuf.at[rem(xx, 2), :, p, div(xx, 2), r_, lanes]

    def wx(d, far, sending):
        to = dev(xx=xr1 if d == 0 else xl1)
        if not far:
            src = x if sending else (xl1 if d == 0 else xr1)
            blk = wblk(src, y, 0)
        else:
            src = (xl1 if d == 0 else xr1) if sending else x2
            blk = wblk(src, y, 0, (d * 224, 224))
        i = 2 * far + d
        return rc(blk, blk, wxs.at[i], wxr.at[i], to)

    def wy(j, d, far, sending):
        xx = rem(x + j, 4)
        to = dev(yy=yr1 if d == 0 else yl1)
        if not far:
            src = y if sending else (yl1 if d == 0 else yr1)
            blk = wblk(xx, src, 0)
        else:
            src = (yl1 if d == 0 else yr1) if sending else y2
            blk = wblk(xx, src, 0, (d * 224, 224))
        i = 2 * far + d
        return rc(blk, blk, wys.at[j, i], wyr.at[j, i], to)

    def wd(j):
        xx = rem(x + j, 4)
        src = wbuf.at[rem(xx, 2), :, 0, div(xx, 2), :, :]
        dst = wbuf.at[rem(xx, 2), :, 1, div(xx, 2), :, :]
        return rc(src, dst, wds.at[j], wdr.at[j], sib)

    def hsend(d, sending):
        rows = pl.ds(d * 224, 224)
        dst = ht.at[h if sending else 1 - h, rows, :]
        return rc(hts.at[rows, :], dst, hss.at[d], hsr.at[d], dev(xx=x2))

    def gd(q, f):
        return rc(gs.at[q, f], gr.at[q, f], ds_.at[q, f], dr.at[q, f], sib)

    def gyfar(q, f):
        return rc(
            yfs.at[q, f], yfr.at[q, f], yf_s.at[q, f], yf_r.at[q, f], dev(yy=yr1 if f == 0 else yl1)
        )

    def gynear(q, d):
        return rc(
            yns.at[q, d], ynr.at[q, d], yn_s.at[q, d], yn_r.at[q, d], dev(yy=yr1 if d == 0 else yl1)
        )

    def lanes(yy):
        return pl.ds(pl.multiple_of(yy * 128, 128), 128)

    def gradient_chunk(kc):
        q = div(kc, 2)
        part = kc - 2 * q
        for d in (0, 1):
            zcopy(d, kc, 3, False).wait_recv()

        @pl.when(part == 0)
        def _():
            def body(f, c):
                gs[q, f] = jnp.dot(ht[f], cbuf[kc], preferred_element_type=F32)
                gd(q, f).start()
                return c

            lax.fori_loop(0, 2, body, 0)

        @pl.when(part == 1)
        def _():
            for f in (0, 1):
                gd(q, f).wait_recv()
                gr[q, f] = gr[q, f] + jnp.dot(ht[f], cbuf[kc], preferred_element_type=F32)
                yfs[q, f] = gr[q, f, :, lanes(y2)].astype(BF16)
                gyfar(q, f).start()

    def ystep2(q):
        gyfar(q, 0).wait_recv()
        yns[q, 0, 0] = (gr[q, 0, :, lanes(yr1)] + yfr[q, 0].astype(F32)).astype(BF16)
        yns[q, 0, 1] = gr[q, 1, :, lanes(yr1)].astype(BF16)
        gynear(q, 0).start()
        gyfar(q, 1).wait_recv()
        yns[q, 1, 0] = gr[q, 0, :, lanes(yl1)].astype(BF16)
        yns[q, 1, 1] = (gr[q, 1, :, lanes(yl1)] + yfr[q, 1].astype(F32)).astype(BF16)
        gynear(q, 1).start()

    def xsend(q, i, sending):
        half = q % 2
        if q < 2:
            return rc(xs.at[q, 0], xr.at[half, 2], x_s.at[q, 0], x_r.at[half, 2], dev(xx=x2))
        if sending:
            return rc(
                xs.at[q, i], xr.at[half, h], x_s.at[q, i], x_r.at[half, h], dev(xx=i * 2 + 1 - xlo)
            )
        return rc(xs.at[q, i], xr.at[half, i], x_s.at[q, i], x_r.at[half, i], dev(xx=x2))

    def ystep3(q):
        for d in (0, 1):
            gynear(q, d).wait_recv()

        def total(f):
            return (
                gr[q, f, :, lanes(y)] + ynr[q, 0, f].astype(F32) + ynr[q, 1, f].astype(F32)
            )

        if q < 2:
            ga[q] = total(h)
            xs[q, 0] = total(1 - h).astype(BF16)
            xsend(q, 0, True).start()
        else:
            for f in (0, 1):
                xs[q, f] = total(f).astype(BF16)
                xsend(q, f, True).start()

    def hg_tile(k, f, toks):
        u = div(k, 2)
        r, half, p = div(u, 2), rem(u, 2), 1 - rem(k, 2)
        w = wbuf[xlo + r - 2 * xlo * r, half, p, f]
        return lax.dot_general(w, cbuf[k, toks, :], NT, preferred_element_type=F32)

    def tile(i):
        return div(i, 4), pl.ds(pl.multiple_of(rem(i, 4) * 256, 256), 256)

    def hg_first():
        def body(i, c):
            f, toks = tile(i)
            acc[f, :, toks] = hg_tile(0, f, toks) + hg_tile(1, f, toks)
            return c

        lax.fori_loop(0, 8, body, 0)

    def hg_add(k):
        k = jnp.int32(k)

        def body(i, c):
            f, toks = tile(i)
            acc[f, :, toks] = acc[f, :, toks] + hg_tile(k, f, toks) + hg_tile(k + 1, f, toks)
            return c

        lax.fori_loop(0, 8, body, 0)

    def hg_one(k):
        def body(i, c):
            f, toks = tile(i)
            acc[f, :, toks] = acc[f, :, toks] + hg_tile(k, f, toks)
            return c

        lax.fori_loop(0, 8, body, 0)

    def hg_last(f):
        def body(i, c):
            toks = tile(i)[1]
            a = hg_tile(jnp.int32(5), f, toks) + hg_tile(jnp.int32(6), f, toks)
            a += hg_tile(jnp.int32(7), f, toks)
            hgs[f, :, toks] = (acc[f, :, toks] + a).astype(BF16)
            return c

        lax.fori_loop(0, 4, body, 0)

    def hgout(t, par):
        return hg_out.at[:, pl.ds(pl.multiple_of((2 * t + par) * 128, 128), 128)]

    def hgsend(t, sending):
        src = hgs.at[1 - h, :, pl.ds(t * 128, 128)]
        dst = hgout(t, h if sending else 1 - h)
        return rc(src, dst, g_s.at[t], g_r.at[t], dev(xx=x2))

    def own_hg_copy():
        for t in range(8):
            src = hgs.at[h, :, pl.ds(t * 128, 128)]
            pltpu.make_async_copy(src, hgout(t, h), lsem.at[4]).start()

    zown(jnp.int32(0))
    zown(jnp.int32(1))
    loads[0].wait()
    for half in (0, 1):
        wbuf[xlo, half, 0, h, :, lanes(y)] = masb[:, half * 128 : half * 128 + 128].astype(BF16)
    wx(0, 0, True).start()
    wx(1, 0, True).start()
    wy(0, 0, 0, True).start()
    wy(0, 1, 0, True).start()
    pltpu.make_async_copy(hts, ht.at[h], lsem.at[4]).wait()

    def tick(s, c):
        zring(s)

        @pl.when(s == 2)
        def _():
            for d in (0, 1):
                wx(d, 0, False).wait_recv()
            for d in (0, 1):
                wx(d, 1, True).start()
            for j in (1, 3):
                for d in (0, 1):
                    wy(j, d, 0, True).start()
            pltpu.make_async_copy(hts, hts, lsem.at[3]).wait()
            for d in (0, 1):
                hsend(d, True).start()

        @pl.when(s == 3)
        def _():
            for d in (0, 1):
                wx(d, 1, False).wait_recv()
            for d in (0, 1):
                wy(2, d, 0, True).start()

        @pl.when(s == 4)
        def _():
            for j in range(4):
                for d in (0, 1):
                    wy(j, d, 0, False).wait_recv()
                    wy(j, d, 1, True).start()

        @pl.when(s == 5)
        def _():
            for d in (0, 1):
                hsend(d, False).wait_recv()
            gradient_chunk(jnp.int32(0))
            for j in range(4):
                for d in (0, 1):
                    wy(j, d, 1, False).wait_recv()
                wd(j).start()

        @pl.when(s == 6)
        def _():
            gradient_chunk(jnp.int32(1))

        @pl.when(s >= 6)
        def _():
            gradient_chunk(s - 4)

        for q in range(3):

            @pl.when(s == (7, 8, 10)[q])
            def _(q=q):
                ystep2(q)

        for q in range(2):

            @pl.when(s == (8, 9)[q])
            def _(q=q):
                ystep3(q)

        @pl.when(s == 6)
        def _():
            for j in range(4):
                wd(j).wait_recv()
            hg_first()

        @pl.when(s == 7)
        def _():
            hg_add(2)

        @pl.when(s == 8)
        def _():
            hg_one(jnp.int32(4))

        return c

    lax.fori_loop(1, 12, tick, 0)

    hg_last(1 - h)
    ystep2(3)
    for t in range(2):
        hgsend(t, True).start()
    ystep3(2)
    hg_last(h)
    own_hg_copy()
    ystep3(3)
    loads[1].wait()
    loads[2].wait()
    sq = jnp.zeros((8, 128), F32)
    gt = []
    for half in (0, 1):
        xsend(half, 0, False).wait_recv()
        for i in (0, 1):
            xsend(2 + half, i, False).wait_recv()
        g = (
            ga[half]
            + xr[half, 2].astype(F32)
            + xr[half, 0].astype(F32)
            + xr[half, 1].astype(F32)
        )
        ga[half] = g
        sq = sq + jnp.sum((g * g).reshape(FC // 8, 8, 128), axis=0)

    groups = [
        [dev(cc=1 - core)]
        + [dev(xx=rem(x + i, 4), cc=c_) for i in (1, 2, 3) for c_ in (core, 1 - core)],
        [dev(yy=rem(y + i, 4)) for i in (1, 2, 3)],
        [dev(zz=rem(z + i, 8)) for i in range(1, 8)],
    ]
    sends = []
    for ph, group in enumerate(groups):
        ns[ph] = sq
        cps = [
            rc(ns.at[ph], nr.at[ph, i], n_s.at[ph, i], n_r.at[ph, i], to)
            for i, to in enumerate(group)
        ]
        for cp in cps:
            cp.start()
        sends += cps
        for i, cp in enumerate(cps):
            cp.wait_recv()
            sq = sq + nr[ph, i]
        if ph == 0:
            for t in range(2, 5):
                hgsend(t, True).start()
    squares = jnp.sum(sq, keepdims=True)
    scale = jnp.minimum(1.0, 1.0 / (jnp.sqrt(squares) + 1e-06))

    for half in (0, 1):
        cols = pl.ds(half * 128, 128)
        clipped = scale * ga[half]
        nm1 = 0.9 * m1b[:, cols] + 0.1 * clipped
        nm2 = 0.95 * m2b[:, cols] + 0.05 * clipped * clipped
        first_hat = nm1 / (1.0 - 0.9**10)
        second_hat = nm2 / (1.0 - 0.95**10)
        w = masb[:, cols]
        nmas = w - 0.01 * (first_hat / (jnp.sqrt(second_hat) + 1e-08) + 0.1 * w)
        m1b[:, cols] = nm1
        m2b[:, cols] = nm2
        masb[:, cols] = nmas
        nwb[:, pl.ds(pl.multiple_of(dp * 256 + half * 128, 128), 128)] = nmas.astype(BF16)

    def nblk(yy, j, half=None, cc=core):
        xl_ = 1 - xlo if j else xlo
        off = ((yy * 2 + xl_) * 2 + cc) * 256
        rows = slice(None) if half is None else pl.ds(half * 224, 224)
        return nwb.at[rows, pl.ds(pl.multiple_of(off, 256), 256)]

    def cp(src, dst, i, to):
        return rc(src, dst, o_s.at[i], o_r.at[i], to)

    to_y = (dev(yy=yr1), dev(yy=yl1))
    from_y = (yl1, yr1)
    to_x = dev(xx=h * 2 + 1 - xlo)
    outs, puts = [], []

    def go(c):
        c.start()
        outs.append(c)

    def put(yy, j, cc=core):
        off = pl.multiple_of(((yy * 2 + (1 - xlo if j else xlo)) * 2 + cc) * 256, 256)
        c = pltpu.make_async_copy(
            nblk(yy, j, cc=cc), nw_out.at[:, pl.ds(off, 256)], w_s.at[len(puts)]
        )
        c.start()
        puts.append(c)

    def await_(blk, i):
        cp(blk, blk, i, sib).wait_recv()

    go(cp(nblk(y, 0), nblk(y, 0), 8, to_x))
    for d in (0, 1):
        go(cp(nblk(y, 0), nblk(y, 0), d, to_y[d]))
    go(cp(nblk(y, 0), nblk(y, 0), 9, sib))
    put(y, 0)
    finals = [
        pltpu.make_async_copy(masb, nm_out, lsem.at[1]),
        pltpu.make_async_copy(m1b, n1_out, lsem.at[2]),
        pltpu.make_async_copy(m2b, n2_out, lsem.at[3]),
    ]
    for c in finals:
        c.start()
    for d in (0, 1):
        b = nblk(from_y[d], 0)
        await_(b, d)
        part = nblk(from_y[d], 0, d)
        go(cp(part, part, 4 + d, to_y[d]))
        go(cp(b, b, 11 + d, sib))
        put(from_y[d], 0)
    b = nblk(y, 1)
    await_(b, 8)
    for d in (0, 1):
        go(cp(b, b, 2 + d, to_y[d]))
    go(cp(b, b, 10, sib))
    put(y, 1)
    for t in range(5, 8):
        hgsend(t, True).start()
    b = nblk(y2, 0)
    for d in (0, 1):
        await_(nblk(y2, 0, d), 4 + d)
    go(cp(b, b, 6, to_x))
    go(cp(b, b, 15, sib))
    put(y2, 0)
    for d in (0, 1):
        b = nblk(from_y[d], 1)
        await_(b, 2 + d)
        go(cp(b, b, 13 + d, sib))
        put(from_y[d], 1)
    b = nblk(y2, 1)
    await_(b, 6)
    go(cp(b, b, 16, sib))
    put(y2, 1)
    oc = 1 - core
    for i, (yy, j) in enumerate(
        ((y, 0), (y, 1), (yl1, 0), (yr1, 0), (yl1, 1), (yr1, 1), (y2, 0), (y2, 1))
    ):
        await_(nblk(yy, j, cc=oc), 9 + i)
        put(yy, j, oc)

    for t in range(8):
        hgsend(t, False).wait_recv()
    pltpu.make_async_copy(hts, hts, lsem.at[4]).wait()
    for c in finals + puts:
        c.wait()
    for c in outs + sends:
        c.wait_send()
    for d in (0, 1):
        hsend(d, True).wait_send()
        for far in (0, 1):
            wx(d, far, True).wait_send()
            for j in range(4):
                wy(j, d, far, True).wait_send()
    for j in range(4):
        wd(j).wait_send()
    for t in range(8):
        hgsend(t, True).wait_send()
    for q in range(4):
        for f in (0, 1):
            gd(q, f).wait_send()
            gyfar(q, f).wait_send()
            gynear(q, f).wait_send()
            if q >= 2 or f == 0:
                xsend(q, f, True).wait_send()

    def drain(k, c):
        for hop in range(4):
            for d in (0, 1):
                zcopy(d, k, hop, True).wait_send()
        return c

    lax.fori_loop(0, NK, drain, 0)


def local(hidden, cotangent, master, moment_one, moment_two):
    dma = pltpu.SemaphoreType.DMA
    any_ = pl.BlockSpec(memory_space=pl.ANY)
    v = pltpu.VMEM
    scratch = [
        v((NK, 1024, 512), BF16),
        v((2, 2, 2, 2, FC, 512), BF16),
        v((2, FC, 1024), BF16),
        v((FC, 1024), BF16),
        v((4, 2, FC, 512), F32),
        v((4, 2, FC, 512), F32),
        v((4, 2, FC, 128), BF16),
        v((4, 2, FC, 128), BF16),
        v((4, 2, 2, FC, 128), BF16),
        v((4, 2, 2, FC, 128), BF16),
        v((4, 2, FC, 128), BF16),
        v((2, 3, FC, 128), BF16),
        v((2, FC, 128), F32),
        v((2, FC, 1024), F32),
        v((2, FC, 1024), BF16),
        v((FC, 256), F32),
        v((FC, 256), F32),
        v((FC, 256), F32),
        v((FC, 4096), BF16),
        v((3, 8, 128), F32),
        v((3, 7, 8, 128), F32),
        dma((5,)),
        dma((NK,)),
        dma((2, NK, 4)), dma((2, NK, 4)),
        dma((2,)), dma((2,)),
        dma((4,)), dma((4,)),
        dma((4, 4)), dma((4, 4)),
        dma((4,)), dma((4,)),
        dma((4, 2)), dma((4, 2)),
        dma((4, 2)), dma((4, 2)),
        dma((4, 2)), dma((4, 2)),
        dma((4, 2)), dma((2, 3)),
        dma((8,)), dma((8,)),
        dma((3, 7)), dma((3, 7)),
        dma((17,)), dma((17,)),
        dma((16,)),
    ]
    sds = jax.ShapeDtypeStruct
    hg, nw, nm, n1, n2 = pl.pallas_call(
        kernel,
        out_shape=(
            sds((FC, 2048), BF16),
            sds((FC, 4096), BF16),
            sds((FC, 256), F32),
            sds((FC, 256), F32),
            sds((FC, 256), F32),
        ),
        in_specs=[any_] * 5,
        out_specs=(any_,) * 5,
        scratch_shapes=scratch,
        compiler_params=pltpu.CompilerParams(
            collective_id=0, has_side_effects=True, vmem_limit_bytes=63 * 2**20
        ),
        cost_estimate=pl.CostEstimate(
            flops=15_032_385_536, bytes_accessed=16_000_000, transcendentals=0
        ),
        name="fused_backward",
    )(hidden.T, cotangent, master.T, moment_one.T, moment_two.T)
    outs = (hg, nw, nm, n1, n2)
    hg, nw, nm, n1, n2 = pl.pallas_call(
        hand_on,
        out_shape=tuple(sds(t.shape, t.dtype) for t in outs),
        in_specs=[any_] * 5,
        out_specs=(any_,) * 5,
        scratch_shapes=[v(t.shape, t.dtype) for t in outs] + [dma((2, 11))],
        compiler_params=pltpu.CompilerParams(vmem_limit_bytes=60 * 2**20),
        name="hand_on",
    )(*outs)
    return (hg.T, nw.T, nm.T, n1.T, n2.T)


def hand_on(*refs):
    srcs, dsts, bufs, sems = refs[:5], refs[5:10], refs[10:15], refs[15]
    ins, outs = [], []
    for src, dst, buf in zip(srcs, dsts, bufs):
        n = 4 if src.shape[1] > 256 else 1
        rows = FC // n
        for i in range(n):
            cut = pl.ds(i * rows, rows)
            k = len(ins)
            ins.append(pltpu.make_async_copy(src.at[cut, :], buf.at[cut, :], sems.at[0, k]))
            outs.append(pltpu.make_async_copy(buf.at[cut, :], dst.at[cut, :], sems.at[1, k]))
    for c in ins:
        c.start()
    for c, d in zip(ins, outs):
        c.wait()
        d.start()
    for d in outs:
        d.wait()


def solution(mesh):
    return jax.shard_map(
        local,
        mesh=mesh,
        in_specs=(
            P("dp", "mp"),
            P(("dp", "mp"), None),
            P("dp", "mp"),
            P("dp", "mp"),
            P("dp", "mp"),
        ),
        out_specs=(P("dp", "mp"), P(None, "mp"), P("dp", "mp"), P("dp", "mp"), P("dp", "mp")),
        check_vma=False,
    )
```

```python
import functools

import jax
import jax.numpy as jnp
from jax import lax
from jax.experimental import pallas as pl
from jax.experimental.pallas import tpu as pltpu
from jax.sharding import PartitionSpec as P

F32 = jnp.float32
BF16 = jnp.bfloat16
NT = (((1,), (1,)), ((), ()))
MESH = pl.DeviceIdType.MESH
FC = 448
NK = 8


def rem(a, n):
    return lax.rem(a, jnp.int32(n))


def div(a, n):
    return lax.div(a, jnp.int32(n))


def kernel(
    hid, cot, mas, m1, m2,
    hg_out, nw_out, nm_out, n1_out, n2_out,
    cbuf, wbuf, ht, hts, gs, gr,
    yfs, yfr, yns, ynr, xs, xr, ga, acc, hgs,
    masb, m1b, m2b, nwb, ns, nr,
    lsem, csem, zs, zr, hss, hsr, wxs, wxr, wys, wyr, wds, wdr,
    ds_, dr, yf_s, yf_r, yn_s, yn_r, x_s, x_r, g_s, g_r, n_s, n_r, o_s, o_r, w_s,
):
    dp = lax.axis_index("dp")
    mp = lax.axis_index("mp")
    core = rem(dp, 2)
    xlo = rem(div(dp, 2), 2)
    y = div(dp, 4)
    h = rem(mp, 2)
    z = div(mp, 2)
    x = h * 2 + xlo
    xr1, xl1, x2 = rem(x + 1, 4), rem(x + 3, 4), rem(x + 2, 4)
    yr1, yl1, y2 = rem(y + 1, 4), rem(y + 3, 4), rem(y + 2, 4)

    def dev(xx=x, yy=y, zz=z, cc=core):
        return ((yy * 2 + rem(xx, 2)) * 2 + cc, zz * 2 + div(xx, 2))

    def rc(src, dst, ss, rs, to):
        return pltpu.make_async_remote_copy(
            src_ref=src, dst_ref=dst, send_sem=ss, recv_sem=rs, device_id=to, device_id_type=MESH
        )

    sib = dev(cc=1 - core)

    loads = [
        pltpu.make_async_copy(mas, masb, lsem.at[0]),
        pltpu.make_async_copy(m1, m1b, lsem.at[1]),
        pltpu.make_async_copy(m2, m2b, lsem.at[2]),
    ]
    zrow = pl.multiple_of(z * 128, 128)
    for k in range(NK):
        q, p = k // 2, 1 - k % 2
        r, half = q // 2, q % 2
        xl_ = 1 - xlo if r else xlo
        c_ = 1 - core if p else core
        for yy in range(4):
            off = pl.multiple_of(((yy * 2 + xl_) * 2 + c_) * 256 + half * 128, 128)
            pltpu.make_async_copy(
                cot.at[:, pl.ds(off, 128)],
                cbuf.at[k, pl.ds(zrow, 128), pl.ds(yy * 128, 128)],
                csem.at[k],
            ).start()
        if k == 0:
            loads[0].start()
            for par, sem in ((1 - h, 3), (h, 4)):
                for t in range(8):
                    src = hid.at[:, pl.ds(pl.multiple_of((2 * t + par) * 128, 128), 128)]
                    dst = hts if sem == 3 else ht.at[h]
                    dst = dst.at[:, pl.ds(t * 128, 128)]
                    pltpu.make_async_copy(src, dst, lsem.at[sem]).start()
    loads[1].start()
    loads[2].start()

    barrier = pltpu.get_barrier_semaphore()
    peers = [sib]
    plane = [
        dev(xx=rem(x + i, 4), yy=rem(y + j, 4), cc=1 - core if c else core)
        for j in range(4) for i in range(4) for c in (0, 1) if i + j + c
    ]
    peers = list(plane)
    peers += [dev(zz=rem(z + i, 8)) for i in range(1, 8)]
    for to in peers:
        pl.semaphore_signal(barrier, inc=1, device_id=to, device_id_type=MESH)
    pl.semaphore_wait(barrier, len(peers))

    zto = (dev(zz=rem(z + 1, 8)), dev(zz=rem(z + 7, 8)))

    def zcopy(d, k, hop):
        slot = rem(z + 16 - hop, 8) if d == 0 else rem(z + hop, 8)
        row, n = slot * 128, 128
        if hop == 3:
            n = 64
            row = row + 64 * d
        ref = cbuf.at[k, pl.ds(pl.multiple_of(row, 64), n), :]
        return rc(ref, ref, zs, zr.at[k, hop], zto[d])

    def zown(k):
        own = cbuf.at[k, pl.ds(zrow, 128), :]
        pltpu.make_async_copy(own, own, csem.at[k]).wait()
        for d in (0, 1):
            zcopy(d, k, 0).start()

    def got(ref, sem):
        pltpu.make_async_copy(ref, ref, sem).wait()

    def zwait(k, hop):
        got(cbuf.at[k, pl.ds(0, 256 if hop < 3 else 128), :], zr.at[k, hop])

    def zring(s):
        for hop in (3, 2, 1):
            k = s - hop

            @pl.when((k >= 0) & (k < NK))
            def _(hop=hop, k=k):
                zwait(k, hop - 1)
                for d in (0, 1):
                    zcopy(d, k, hop).start()

        @pl.when(s < NK - 1)
        def _():
            zown(s + 1)

    def wblk(xx, yy, p, rows=None):
        lanes = pl.ds(pl.multiple_of(yy * 128, 128), 128)
        r_ = slice(None) if rows is None else pl.ds(rows[0], rows[1])
        return wbuf.at[rem(xx, 2), :, p, div(xx, 2), r_, lanes]

    def wx(d, far):
        src = x if not far else (xl1 if d == 0 else xr1)
        blk = wblk(src, y, 0, (d * 224, 224) if far else None)
        return rc(blk, blk, wxs, wxr.at[far], dev(xx=xr1 if d == 0 else xl1))

    def wy(j, d, far):
        src = y if not far else (yl1 if d == 0 else yr1)
        blk = wblk(rem(x + j, 4), src, 0, (d * 224, 224) if far else None)
        return rc(blk, blk, wys, wyr.at[far], dev(yy=yr1 if d == 0 else yl1))

    def wd(j):
        xx = rem(x + j, 4)
        src = wbuf.at[rem(xx, 2), :, 0, div(xx, 2), :, :]
        dst = wbuf.at[rem(xx, 2), :, 1, div(xx, 2), :, :]
        return rc(src, dst, wds, wdr, sib)

    def hsend(d):
        rows = pl.ds(d * 224, 224)
        dst = ht.at[h, rows, :]
        return rc(hts.at[rows, :], dst, hss, hsr, dev(xx=x2))

    def gd(q, f):
        return rc(gs.at[q, f], gr.at[q, f], ds_, dr.at[q, f], sib)

    def gyfar(q, f):
        return rc(
            yfs.at[q, f], yfr.at[q, f], yf_s, yf_r.at[q, f], dev(yy=yr1 if f == 0 else yl1)
        )

    def gynear(q, d, f):
        return rc(
            yns.at[q, d, f], ynr.at[q, d, f], yn_s, yn_r.at[q],
            dev(yy=yr1 if d == 0 else yl1),
        )

    def lanes(yy):
        return pl.ds(pl.multiple_of(yy * 128, 128), 128)

    def gradient_chunk(kc):
        q = div(kc, 2)
        part = kc - 2 * q
        zwait(kc, 3)

        @pl.when(part == 0)
        def _():
            def body(f, c):
                gs[q, f] = jnp.dot(ht[f], cbuf[kc], preferred_element_type=F32)
                gd(q, f).start()
                return c

            lax.fori_loop(0, 2, body, 0)

        @pl.when(part == 1)
        def _():
            for f in (0, 1):
                gd(q, f).wait_recv()
                gr[q, f] = gr[q, f] + jnp.dot(ht[f], cbuf[kc], preferred_element_type=F32)
                yfs[q, f] = gr[q, f, :, lanes(y2)].astype(BF16)
                gyfar(q, f).start()
            for f in (1, 0):
                yns[q, 1 - f, f] = gr[q, f, :, lanes(yl1 if f == 0 else yr1)].astype(BF16)
                gynear(q, 1 - f, f).start()

    def ystep2(q):
        for f in (0, 1):
            gyfar(q, f).wait_recv()
            own = gr[q, f, :, lanes(yr1 if f == 0 else yl1)]
            yns[q, f, f] = (own + yfr[q, f].astype(F32)).astype(BF16)
            gynear(q, f, f).start()

    def xsend(q, i):
        half = q % 2
        if q < 2:
            return rc(xs.at[q, 0], xr.at[half, 2], x_s, x_r, dev(xx=x2))
        return rc(xs.at[q, i], xr.at[half, h], x_s, x_r, dev(xx=i * 2 + 1 - xlo))

    def ystep3(q):
        got(ynr.at[q], yn_r.at[q])

        def total(f):
            return (
                gr[q, f, :, lanes(y)] + ynr[q, 0, f].astype(F32) + ynr[q, 1, f].astype(F32)
            )

        if q < 2:
            ga[q] = total(h)
            xs[q, 0] = total(1 - h).astype(BF16)
            xsend(q, 0).start()
        else:
            for f in (0, 1):
                xs[q, f] = total(f).astype(BF16)
                xsend(q, f).start()

    def hg_tile(k, f, toks):
        u = div(k, 2)
        r, half, p = div(u, 2), rem(u, 2), 1 - rem(k, 2)
        w = wbuf[xlo + r - 2 * xlo * r, half, p, f]
        return lax.dot_general(w, cbuf[k, toks, :], NT, preferred_element_type=F32)

    def tile(i):
        return div(i, 4), pl.ds(pl.multiple_of(rem(i, 4) * 256, 256), 256)

    def hg_first():
        def body(i, c):
            f, toks = tile(i)
            acc[f, :, toks] = hg_tile(0, f, toks) + hg_tile(1, f, toks)
            return c

        lax.fori_loop(0, 8, body, 0)

    def hg_add(k):
        k = jnp.int32(k)

        def body(i, c):
            f, toks = tile(i)
            acc[f, :, toks] = acc[f, :, toks] + hg_tile(k, f, toks) + hg_tile(k + 1, f, toks)
            return c

        lax.fori_loop(0, 8, body, 0)

    def hg_one(k):
        def body(i, c):
            f, toks = tile(i)
            acc[f, :, toks] = acc[f, :, toks] + hg_tile(k, f, toks)
            return c

        lax.fori_loop(0, 8, body, 0)

    def hg_last(f):
        def body(i, c):
            toks = tile(i)[1]
            a = hg_tile(jnp.int32(5), f, toks) + hg_tile(jnp.int32(6), f, toks)
            a += hg_tile(jnp.int32(7), f, toks)
            hgs[f, :, toks] = (acc[f, :, toks] + a).astype(BF16)
            return c

        lax.fori_loop(0, 4, body, 0)

    def hgout(t, par):
        return hg_out.at[:, pl.ds(pl.multiple_of((2 * t + par) * 128, 128), 128)]

    def hgsend(t):
        src = hgs.at[1 - h, :, pl.ds(t * 128, 128)]
        dst = hgout(t, h)
        return rc(src, dst, g_s, g_r, dev(xx=x2))

    def own_hg_copy():
        for t in range(8):
            src = hgs.at[h, :, pl.ds(t * 128, 128)]
            pltpu.make_async_copy(src, hgout(t, h), lsem.at[4]).start()

    zown(jnp.int32(0))
    zown(jnp.int32(1))
    loads[0].wait()
    for half in (0, 1):
        wbuf[xlo, half, 0, h, :, lanes(y)] = masb[:, half * 128 : half * 128 + 128].astype(BF16)
    wx(0, 0).start()
    wx(1, 0).start()
    wy(0, 0, 0).start()
    wy(0, 1, 0).start()
    pltpu.make_async_copy(hts, ht.at[h], lsem.at[4]).wait()

    def tick(s, c):
        zring(s)

        @pl.when(s == 1)
        def _():
            got(gs.at[0, 0, pl.ds(0, 224), :], wxr.at[0])
            for d in (0, 1):
                wx(d, 1).start()
            for j in (1, 3):
                for d in (0, 1):
                    wy(j, d, 0).start()

        @pl.when(s == 2)
        def _():
            got(gs.at[0, 0, pl.ds(0, 112), :], wxr.at[1])
            for d in (0, 1):
                wy(2, d, 0).start()
            pltpu.make_async_copy(hts, hts, lsem.at[3]).wait()
            for d in (0, 1):
                hsend(d).start()

        @pl.when(s == 4)
        def _():
            got(gs.at[0], wyr.at[0])
            for j in range(4):
                for d in (0, 1):
                    wy(j, d, 1).start()

        @pl.when(s == 5)
        def _():
            got(hts, hsr)
            gradient_chunk(jnp.int32(0))
            got(gs.at[0, 0], wyr.at[1])
            for j in range(4):
                wd(j).start()

        @pl.when(s == 6)
        def _():
            gradient_chunk(jnp.int32(1))

        @pl.when(s >= 6)
        def _():
            gradient_chunk(s - 4)

        for q in range(3):

            @pl.when(s == (7, 8, 10)[q])
            def _(q=q):
                ystep2(q)

        for q in range(2):

            @pl.when(s == (8, 9)[q])
            def _(q=q):
                ystep3(q)

        @pl.when(s == 6)
        def _():
            got(gs.at[:, 0], wdr)
            hg_first()

        @pl.when(s == 7)
        def _():
            hg_add(2)

        @pl.when(s == 8)
        def _():
            hg_one(jnp.int32(4))

        return c

    lax.fori_loop(1, 12, tick, 0)

    hg_last(1 - h)
    for t in range(2):
        hgsend(t).start()
    ystep2(3)
    ystep3(2)
    hg_last(h)
    own_hg_copy()
    ystep3(3)
    loads[1].wait()
    loads[2].wait()
    sq = jnp.zeros((8, 128), F32)
    got(xr, x_r)
    for half in (0, 1):
        g = (
            ga[half]
            + xr[half, 2].astype(F32)
            + xr[half, 0].astype(F32)
            + xr[half, 1].astype(F32)
        )
        ga[half] = g
        sq = sq + jnp.sum((g * g).reshape(FC // 8, 8, 128), axis=0)

    groups = [plane, [dev(zz=rem(z + i, 8)) for i in range(1, 8)]]
    base = 0
    for ph, group in enumerate(groups):
        ns[ph] = sq
        for i, to in enumerate(group):
            rc(ns.at[ph], nr.at[base + i], n_s, n_r.at[ph], to).start()
        if ph == 1:
            for t in range(2, 5):
                hgsend(t).start()
        heard = nr.at[pl.ds(base, len(group))]
        got(heard, n_r.at[ph])
        sq = sq + jnp.sum(heard[...], axis=0)
        base += len(group)
    squares = jnp.sum(sq, keepdims=True)
    scale = jnp.minimum(1.0, 1.0 / (jnp.sqrt(squares) + 1e-06))

    for half in (0, 1):
        cols = pl.ds(half * 128, 128)
        clipped = scale * ga[half]
        nm1 = 0.9 * m1b[:, cols] + 0.1 * clipped
        nm2 = 0.95 * m2b[:, cols] + 0.05 * clipped * clipped
        first_hat = nm1 / (1.0 - 0.9**10)
        second_hat = nm2 / (1.0 - 0.95**10)
        w = masb[:, cols]
        nmas = w - 0.01 * (first_hat / (jnp.sqrt(second_hat) + 1e-08) + 0.1 * w)
        m1b[:, cols] = nm1
        m2b[:, cols] = nm2
        masb[:, cols] = nmas
        nwb[:, pl.ds(pl.multiple_of(dp * 256 + half * 128, 128), 128)] = nmas.astype(BF16)

    def nblk(yy, j, half=None, cc=core):
        xl_ = 1 - xlo if j else xlo
        off = ((yy * 2 + xl_) * 2 + cc) * 256
        rows = slice(None) if half is None else pl.ds(half * 224, 224)
        return nwb.at[rows, pl.ds(pl.multiple_of(off, 256), 256)]

    def cp(src, dst, i, to):
        return rc(src, dst, o_s, o_r.at[i], to)

    to_y = (dev(yy=yr1), dev(yy=yl1))
    from_y = (yl1, yr1)
    to_x = dev(xx=h * 2 + 1 - xlo)

    def go(c):
        c.start()

    def put(yy, j, cc=core):
        off = pl.multiple_of(((yy * 2 + (1 - xlo if j else xlo)) * 2 + cc) * 256, 256)
        c = pltpu.make_async_copy(
            nblk(yy, j, cc=cc), nw_out.at[:, pl.ds(off, 256)], w_s
        )
        c.start()

    def await_(blk, i):
        cp(blk, blk, i, sib).wait_recv()

    go(cp(nblk(y, 0), nblk(y, 0), 8, to_x))
    for d in (0, 1):
        go(cp(nblk(y, 0), nblk(y, 0), d, to_y[d]))
    go(cp(nblk(y, 0), nblk(y, 0), 9, sib))
    put(y, 0)
    finals = [
        pltpu.make_async_copy(masb, nm_out, lsem.at[1]),
        pltpu.make_async_copy(m1b, n1_out, lsem.at[2]),
        pltpu.make_async_copy(m2b, n2_out, lsem.at[3]),
    ]
    for c in finals:
        c.start()
    for d in (0, 1):
        b = nblk(from_y[d], 0)
        await_(b, d)
        part = nblk(from_y[d], 0, d)
        go(cp(part, part, 4 + d, to_y[d]))
        go(cp(b, b, 11 + d, sib))
        put(from_y[d], 0)
    b = nblk(y, 1)
    await_(b, 8)
    for d in (0, 1):
        go(cp(b, b, 2 + d, to_y[d]))
    for t in range(5, 8):
        hgsend(t).start()
    go(cp(b, b, 10, sib))
    put(y, 1)
    b = nblk(y2, 0)
    for d in (0, 1):
        await_(nblk(y2, 0, d), 4 + d)
    go(cp(b, b, 15, sib))
    put(y2, 0)
    for d in (0, 1):
        b = nblk(from_y[d], 1)
        await_(b, 2 + d)
        part = nblk(from_y[d], 1, d)
        go(cp(part, part, 6 + d, to_y[d]))
        go(cp(b, b, 13 + d, sib))
        put(from_y[d], 1)
    b = nblk(y2, 1)
    for d in (0, 1):
        await_(nblk(y2, 1, d), 6 + d)
    go(cp(b, b, 16, sib))
    put(y2, 1)
    oc = 1 - core
    for i, (yy, j) in enumerate(
        ((y, 0), (y, 1), (yl1, 0), (yr1, 0), (yl1, 1), (yr1, 1), (y2, 0), (y2, 1))
    ):
        await_(nblk(yy, j, cc=oc), 9 + i)
        put(yy, j, oc)

    got(hts, g_r)
    got(hts, lsem.at[4])
    for c in finals:
        c.wait()
    got(nwb, w_s)
    got(hts, g_s)
    got(hts, hss)
    got(cbuf.at[pl.ds(0, 7)], zs)
    got(gs.at[0, 0, pl.ds(0, 336), :], wxs)
    got(gs.at[pl.ds(0, 3), 0], wys)
    got(gs.at[:, 0], wds)
    got(gs, ds_)
    got(yfs, yf_s)
    got(yns, yn_s)
    got(xs.at[pl.ds(0, 3)], x_s)
    got(nr, n_s)
    got(nwb.at[:, pl.ds(0, 3840)], o_s)


def local(hidden, cotangent, master, moment_one, moment_two):
    dma = pltpu.SemaphoreType.DMA
    any_ = pl.BlockSpec(memory_space=pl.ANY)
    v = pltpu.VMEM
    scratch = [
        v((NK, 1024, 512), BF16),
        v((2, 2, 2, 2, FC, 512), BF16),
        v((2, FC, 1024), BF16),
        v((FC, 1024), BF16),
        v((4, 2, FC, 512), F32),
        v((4, 2, FC, 512), F32),
        v((4, 2, FC, 128), BF16),
        v((4, 2, FC, 128), BF16),
        v((4, 2, 2, FC, 128), BF16),
        v((4, 2, 2, FC, 128), BF16),
        v((4, 2, FC, 128), BF16),
        v((2, 3, FC, 128), BF16),
        v((2, FC, 128), F32),
        v((2, FC, 1024), F32),
        v((2, FC, 1024), BF16),
        v((FC, 256), F32),
        v((FC, 256), F32),
        v((FC, 256), F32),
        v((FC, 4096), BF16),
        v((2, 8, 128), F32),
        v((38, 8, 128), F32),
        dma((5,)),
        dma((NK,)),
        dma, dma((NK, 4)),
        dma, dma,
        dma, dma((2,)),
        dma, dma((2,)),
        dma, dma,
        dma, dma((4, 2)),
        dma, dma((4, 2)),
        dma, dma((4,)),
        dma, dma,
        dma, dma,
        dma, dma((2,)),
        dma, dma((17,)),
        dma,
    ]
    sds = jax.ShapeDtypeStruct
    hg, nw, nm, n1, n2 = pl.pallas_call(
        kernel,
        out_shape=(
            sds((FC, 2048), BF16),
            sds((FC, 4096), BF16),
            sds((FC, 256), F32),
            sds((FC, 256), F32),
            sds((FC, 256), F32),
        ),
        in_specs=[any_] * 5,
        out_specs=(any_,) * 5,
        scratch_shapes=scratch,
        compiler_params=pltpu.CompilerParams(
            collective_id=0, has_side_effects=True, vmem_limit_bytes=63 * 2**20
        ),
        cost_estimate=pl.CostEstimate(
            flops=15_032_385_536, bytes_accessed=16_000_000, transcendentals=0
        ),
        name="fused_backward",
    )(hidden.T, cotangent, master.T, moment_one.T, moment_two.T)
    outs = (hg, nw, nm, n1, n2)
    hg, nw, nm, n1, n2 = pl.pallas_call(
        hand_on,
        out_shape=tuple(sds(t.shape, t.dtype) for t in outs),
        in_specs=[any_] * 5,
        out_specs=(any_,) * 5,
        scratch_shapes=[v(t.shape, t.dtype) for t in outs] + [dma((2, 11))],
        compiler_params=pltpu.CompilerParams(vmem_limit_bytes=60 * 2**20),
        name="hand_on",
    )(*outs)
    return (hg.T, nw.T, nm.T, n1.T, n2.T)


def hand_on(*refs):
    srcs, dsts, bufs, sems = refs[:5], refs[5:10], refs[10:15], refs[15]
    ins, outs = [], []
    for src, dst, buf in zip(srcs, dsts, bufs):
        n = 4 if src.shape[1] > 256 else 1
        rows = FC // n
        for i in range(n):
            cut = pl.ds(i * rows, rows)
            k = len(ins)
            ins.append(pltpu.make_async_copy(src.at[cut, :], buf.at[cut, :], sems.at[0, k]))
            outs.append(pltpu.make_async_copy(buf.at[cut, :], dst.at[cut, :], sems.at[1, k]))
    for c in ins:
        c.start()
    for c, d in zip(ins, outs):
        c.wait()
        d.start()
    for d in outs:
        d.wait()


def solution(mesh):
    return jax.shard_map(
        local,
        mesh=mesh,
        in_specs=(
            P("dp", "mp"),
            P(("dp", "mp"), None),
            P("dp", "mp"),
            P("dp", "mp"),
            P("dp", "mp"),
        ),
        out_specs=(P("dp", "mp"), P(None, "mp"), P("dp", "mp"), P("dp", "mp"), P("dp", "mp")),
        check_vma=False,
    )
```

```python
import functools

import jax
import jax.numpy as jnp
from jax import lax
from jax.experimental import pallas as pl
from jax.experimental.pallas import tpu as pltpu
from jax.sharding import PartitionSpec as P

F32 = jnp.float32
BF16 = jnp.bfloat16
NT = (((1,), (1,)), ((), ()))
MESH = pl.DeviceIdType.MESH
FC = 448
NK = 8


def rem(a, n):
    return lax.rem(a, jnp.int32(n))


def div(a, n):
    return lax.div(a, jnp.int32(n))


def kernel(
    hid, cot, mas, m1, m2,
    hg_out, nw_out, nm_out, n1_out, n2_out,
    cbuf, wbuf, ht, hts, gs, gr,
    yfs, yfr, yns, ynr, xs, xr, ga, acc, hgs,
    masb, m1b, m2b, nwb, ns, nr,
    lsem, csem, zs, zr, hss, hsr, wxs, wxr, wys, wyr, wds, wdr,
    ds_, dr, yf_s, yf_r, yn_s, yn_r, x_s, x_r, g_s, g_r, n_s, n_r, o_s, o_r, w_s,
):
    dp = lax.axis_index("dp")
    mp = lax.axis_index("mp")
    core = rem(dp, 2)
    xlo = rem(div(dp, 2), 2)
    y = div(dp, 4)
    h = rem(mp, 2)
    z = div(mp, 2)
    x = h * 2 + xlo
    xr1, xl1, x2 = rem(x + 1, 4), rem(x + 3, 4), rem(x + 2, 4)
    yr1, yl1, y2 = rem(y + 1, 4), rem(y + 3, 4), rem(y + 2, 4)

    def dev(xx=x, yy=y, zz=z, cc=core):
        return ((yy * 2 + rem(xx, 2)) * 2 + cc, zz * 2 + div(xx, 2))

    def rc(src, dst, ss, rs, to):
        return pltpu.make_async_remote_copy(
            src_ref=src, dst_ref=dst, send_sem=ss, recv_sem=rs, device_id=to, device_id_type=MESH
        )

    sib = dev(cc=1 - core)

    loads = [
        pltpu.make_async_copy(mas, masb, lsem.at[0]),
        pltpu.make_async_copy(m1, m1b, lsem.at[1]),
        pltpu.make_async_copy(m2, m2b, lsem.at[2]),
    ]
    zrow = pl.multiple_of(z * 128, 128)
    for k in range(NK):
        q, p = k // 2, 1 - k % 2
        r, half = q // 2, q % 2
        xl_ = 1 - xlo if r else xlo
        c_ = 1 - core if p else core
        for yy in range(4):
            off = pl.multiple_of(((yy * 2 + xl_) * 2 + c_) * 256 + half * 128, 128)
            pltpu.make_async_copy(
                cot.at[:, pl.ds(off, 128)],
                cbuf.at[k, pl.ds(zrow, 128), pl.ds(yy * 128, 128)],
                csem.at[k],
            ).start()
        if k == 0:
            loads[0].start()
            for par, sem in ((1 - h, 3), (h, 4)):
                for t in range(8):
                    src = hid.at[:, pl.ds(pl.multiple_of((2 * t + par) * 128, 128), 128)]
                    dst = hts if sem == 3 else ht.at[h]
                    dst = dst.at[:, pl.ds(t * 128, 128)]
                    pltpu.make_async_copy(src, dst, lsem.at[sem]).start()
    loads[1].start()
    loads[2].start()

    barrier = pltpu.get_barrier_semaphore()
    peers = [sib]
    plane = [
        dev(xx=rem(x + i, 4), yy=rem(y + j, 4), cc=1 - core if c else core)
        for j in range(4) for i in range(4) for c in (0, 1) if i + j + c
    ]
    peers = list(plane)
    peers += [dev(zz=rem(z + i, 8)) for i in range(1, 8)]
    for to in peers:
        pl.semaphore_signal(barrier, inc=1, device_id=to, device_id_type=MESH)
    pl.semaphore_wait(barrier, len(peers))

    zto = (dev(zz=rem(z + 1, 8)), dev(zz=rem(z + 7, 8)))

    def zcopy(d, k, hop):
        slot = rem(z + 16 - hop, 8) if d == 0 else rem(z + hop, 8)
        row, n = slot * 128, 128
        if hop == 3:
            n = 64
            row = row + 64 * d
        ref = cbuf.at[k, pl.ds(pl.multiple_of(row, 64), n), :]
        return rc(ref, ref, zs, zr.at[k, hop], zto[d])

    def zown(k):
        own = cbuf.at[k, pl.ds(zrow, 128), :]
        pltpu.make_async_copy(own, own, csem.at[k]).wait()
        for d in (0, 1):
            zcopy(d, k, 0).start()

    def got(ref, sem):
        pltpu.make_async_copy(ref, ref, sem).wait()

    def zwait(k, hop):
        got(cbuf.at[k, pl.ds(0, 256 if hop < 3 else 128), :], zr.at[k, hop])

    def zring(s):
        def forward(k, hop):
            zwait(k, hop - 1)
            for d in (0, 1):
                zcopy(d, k, hop).start()

        for hop in (3, 2, 1):

            @pl.when((s >= hop) & (s - hop < NK - 1))
            def _(hop=hop):
                forward(s - hop, hop)

            @pl.when(s - hop == NK - 2)
            def _(hop=hop):
                forward(jnp.int32(NK - 1), hop)

        @pl.when(s < NK - 1)
        def _():
            zown(s + 1)

    def wblk(xx, yy, p, rows=None):
        lanes = pl.ds(pl.multiple_of(yy * 128, 128), 128)
        r_ = slice(None) if rows is None else pl.ds(rows[0], rows[1])
        return wbuf.at[rem(xx, 2), :, p, div(xx, 2), r_, lanes]

    def wx(d, far):
        src = x if not far else (xl1 if d == 0 else xr1)
        blk = wblk(src, y, 0, (d * 224, 224) if far else None)
        return rc(blk, blk, wxs, wxr.at[far], dev(xx=xr1 if d == 0 else xl1))

    def wy(j, d, far):
        src = y if not far else (yl1 if d == 0 else yr1)
        blk = wblk(rem(x + j, 4), src, 0, (d * 224, 224) if far else None)
        return rc(blk, blk, wys, wyr.at[far], dev(yy=yr1 if d == 0 else yl1))

    def wd(j):
        xx = rem(x + j, 4)
        src = wbuf.at[rem(xx, 2), :, 0, div(xx, 2), :, :]
        dst = wbuf.at[rem(xx, 2), :, 1, div(xx, 2), :, :]
        return rc(src, dst, wds, wdr, sib)

    def hsend(d):
        rows = pl.ds(d * 224, 224)
        dst = ht.at[h, rows, :]
        return rc(hts.at[rows, :], dst, hss, hsr, dev(xx=x2))

    def gd(q, f):
        return rc(gs.at[q, f], gr.at[q, f], ds_, dr.at[q, f], sib)

    def gyfar(q, f):
        return rc(
            yfs.at[q, f], yfr.at[q, f], yf_s, yf_r.at[q, f], dev(yy=yr1 if f == 0 else yl1)
        )

    def gynear(q, d, f):
        return rc(
            yns.at[q, d, f], ynr.at[q, d, f], yn_s, yn_r.at[q],
            dev(yy=yr1 if d == 0 else yl1),
        )

    def lanes(yy):
        return pl.ds(pl.multiple_of(yy * 128, 128), 128)

    def gradient_chunk(kc):
        q = div(kc, 2)
        part = kc - 2 * q
        zwait(kc, 3)

        @pl.when(part == 0)
        def _():
            def body(f, c):
                gs[q, f] = jnp.dot(ht[f], cbuf[kc], preferred_element_type=F32)
                gd(q, f).start()
                return c

            lax.fori_loop(0, 2, body, 0)

        @pl.when(part == 1)
        def _():
            for f in (0, 1):
                own = jnp.dot(ht[f], cbuf[kc], preferred_element_type=F32)
                gd(q, f).wait_recv()
                gr[q, f] = gr[q, f] + own
                yfs[q, f] = gr[q, f, :, lanes(y2)].astype(BF16)
                gyfar(q, f).start()
            for f in (1, 0):
                yns[q, 1 - f, f] = gr[q, f, :, lanes(yl1 if f == 0 else yr1)].astype(BF16)
                gynear(q, 1 - f, f).start()

    def ystep2(q):
        for f in (0, 1):
            gyfar(q, f).wait_recv()
            own = gr[q, f, :, lanes(yr1 if f == 0 else yl1)]
            yns[q, f, f] = (own + yfr[q, f].astype(F32)).astype(BF16)
            gynear(q, f, f).start()

    def xsend(q, i):
        half = q % 2
        if q < 2:
            return rc(xs.at[q, 0], xr.at[half, 2], x_s, x_r, dev(xx=x2))
        return rc(xs.at[q, i], xr.at[half, h], x_s, x_r, dev(xx=i * 2 + 1 - xlo))

    def ystep3(q):
        got(ynr.at[q], yn_r.at[q])

        def total(f):
            return (
                gr[q, f, :, lanes(y)] + ynr[q, 0, f].astype(F32) + ynr[q, 1, f].astype(F32)
            )

        if q < 2:
            ga[q] = total(h)
            xs[q, 0] = total(1 - h).astype(BF16)
            xsend(q, 0).start()
        else:
            for f in (0, 1):
                xs[q, f] = total(f).astype(BF16)
                xsend(q, f).start()

    def hg_tile(k, f, toks):
        u = div(k, 2)
        r, half, p = div(u, 2), rem(u, 2), 1 - rem(k, 2)
        w = wbuf[xlo + r - 2 * xlo * r, half, p, f]
        return lax.dot_general(w, cbuf[k, toks, :], NT, preferred_element_type=F32)

    def tile(i):
        return div(i, 4), pl.ds(pl.multiple_of(rem(i, 4) * 256, 256), 256)

    def hg_first():
        def body(i, c):
            f, toks = tile(i)
            acc[f, :, toks] = hg_tile(0, f, toks) + hg_tile(1, f, toks)
            return c

        lax.fori_loop(0, 8, body, 0)

    def hg_add(k):
        k = jnp.int32(k)

        def body(i, c):
            f, toks = tile(i)
            acc[f, :, toks] = acc[f, :, toks] + hg_tile(k, f, toks) + hg_tile(k + 1, f, toks)
            return c

        lax.fori_loop(0, 8, body, 0)

    def hg_one(k):
        def body(i, c):
            f, toks = tile(i)
            acc[f, :, toks] = acc[f, :, toks] + hg_tile(k, f, toks)
            return c

        lax.fori_loop(0, 8, body, 0)

    def hg_last(f):
        def body(i, c):
            toks = tile(i)[1]
            a = hg_tile(jnp.int32(5), f, toks) + hg_tile(jnp.int32(6), f, toks)
            a += hg_tile(jnp.int32(7), f, toks)
            hgs[f, :, toks] = (acc[f, :, toks] + a).astype(BF16)
            return c

        lax.fori_loop(0, 4, body, 0)

    def hgout(t, par):
        return hg_out.at[:, pl.ds(pl.multiple_of((2 * t + par) * 128, 128), 128)]

    def hgsend(t):
        src = hgs.at[1 - h, :, pl.ds(t * 128, 128)]
        dst = hgout(t, h)
        return rc(src, dst, g_s, g_r, dev(xx=x2))

    def own_hg_copy():
        for t in range(8):
            src = hgs.at[h, :, pl.ds(t * 128, 128)]
            pltpu.make_async_copy(src, hgout(t, h), lsem.at[4]).start()

    zown(jnp.int32(0))
    zown(jnp.int32(1))
    loads[0].wait()
    for half in (0, 1):
        wbuf[xlo, half, 0, h, :, lanes(y)] = masb[:, half * 128 : half * 128 + 128].astype(BF16)
    wx(0, 0).start()
    wx(1, 0).start()
    wy(0, 0, 0).start()
    wy(0, 1, 0).start()
    pltpu.make_async_copy(hts, ht.at[h], lsem.at[4]).wait()

    def tick(s, c):
        @pl.when(s >= 6)
        def _():
            gradient_chunk(s - 4)

        zring(s)

        @pl.when(s == 1)
        def _():
            got(gs.at[0, 0, pl.ds(0, 224), :], wxr.at[0])
            for d in (0, 1):
                wx(d, 1).start()
            for j in (1, 3):
                for d in (0, 1):
                    wy(j, d, 0).start()

        @pl.when(s == 2)
        def _():
            got(gs.at[0, 0, pl.ds(0, 112), :], wxr.at[1])
            for d in (0, 1):
                wy(2, d, 0).start()
            pltpu.make_async_copy(hts, hts, lsem.at[3]).wait()
            for d in (0, 1):
                hsend(d).start()

        @pl.when(s == 4)
        def _():
            got(gs.at[0], wyr.at[0])
            for j in range(4):
                for d in (0, 1):
                    wy(j, d, 1).start()

        @pl.when(s == 5)
        def _():
            got(hts, hsr)
            gradient_chunk(jnp.int32(0))
            got(gs.at[0, 0], wyr.at[1])
            for j in range(4):
                wd(j).start()

        @pl.when(s == 6)
        def _():
            gradient_chunk(jnp.int32(1))

        for q in range(2):

            @pl.when(s == (7, 8)[q])
            def _(q=q):
                ystep2(q)

        for q in range(2):

            @pl.when(s == (8, 9)[q])
            def _(q=q):
                ystep3(q)

        @pl.when(s == 6)
        def _():
            got(gs.at[:, 0], wdr)
            hg_first()

        @pl.when(s == 7)
        def _():
            hg_add(2)

        @pl.when(s == 8)
        def _():
            hg_one(jnp.int32(4))

        return c

    lax.fori_loop(1, 11, tick, 0)

    ystep2(2)
    gradient_chunk(jnp.int32(7))
    hg_last(1 - h)
    ystep3(2)
    for t in range(2):
        hgsend(t).start()
    ystep2(3)
    hg_last(h)
    own_hg_copy()
    ystep3(3)
    loads[1].wait()
    loads[2].wait()
    sq = jnp.zeros((8, 128), F32)
    got(xr, x_r)
    for half in (0, 1):
        g = (
            ga[half]
            + xr[half, 2].astype(F32)
            + xr[half, 0].astype(F32)
            + xr[half, 1].astype(F32)
        )
        ga[half] = g
        sq = sq + jnp.sum((g * g).reshape(FC // 8, 8, 128), axis=0)

    groups = [plane, [dev(zz=rem(z + i, 8)) for i in range(1, 8)]]
    base = 0
    for ph, group in enumerate(groups):
        ns[ph] = jnp.sum(sq, axis=0, keepdims=True)
        for i, to in enumerate(group):
            rc(ns.at[ph], nr.at[base + i], n_s, n_r.at[ph], to).start()
        if ph == 1:
            for t in range(2, 4):
                hgsend(t).start()
        heard = nr.at[pl.ds(base, len(group))]
        got(heard, n_r.at[ph])
        sq = ns[ph] + jnp.sum(heard[...], axis=0)
        base += len(group)
    squares = jnp.sum(sq, keepdims=True)
    scale = jnp.minimum(1.0, 1.0 / (jnp.sqrt(squares) + 1e-06))

    for half in (0, 1):
        cols = pl.ds(half * 128, 128)
        clipped = scale * ga[half]
        nm1 = 0.9 * m1b[:, cols] + 0.1 * clipped
        nm2 = 0.95 * m2b[:, cols] + 0.05 * clipped * clipped
        first_hat = nm1 / (1.0 - 0.9**10)
        second_hat = nm2 / (1.0 - 0.95**10)
        w = masb[:, cols]
        nmas = w - 0.01 * (first_hat / (jnp.sqrt(second_hat) + 1e-08) + 0.1 * w)
        m1b[:, cols] = nm1
        m2b[:, cols] = nm2
        masb[:, cols] = nmas
        nwb[:, pl.ds(pl.multiple_of(dp * 256 + half * 128, 128), 128)] = nmas.astype(BF16)

    def nblk(yy, j, half=None, cc=core):
        xl_ = 1 - xlo if j else xlo
        off = ((yy * 2 + xl_) * 2 + cc) * 256
        rows = slice(None) if half is None else pl.ds(half * 224, 224)
        return nwb.at[rows, pl.ds(pl.multiple_of(off, 256), 256)]

    def cp(src, dst, i, to):
        return rc(src, dst, o_s, o_r.at[i], to)

    to_y = (dev(yy=yr1), dev(yy=yl1))
    from_y = (yl1, yr1)
    to_x = dev(xx=h * 2 + 1 - xlo)

    def go(c):
        c.start()

    def put(yy, j, cc=core):
        off = pl.multiple_of(((yy * 2 + (1 - xlo if j else xlo)) * 2 + cc) * 256, 256)
        c = pltpu.make_async_copy(
            nblk(yy, j, cc=cc), nw_out.at[:, pl.ds(off, 256)], w_s
        )
        c.start()

    def await_(blk, i):
        cp(blk, blk, i, sib).wait_recv()

    for i in (0, 1):
        go(cp(nblk(y, 0, i), nblk(y, 0, i), 8 + 9 * i, to_x))
    for d in (0, 1):
        go(cp(nblk(y, 0), nblk(y, 0), d, to_y[d]))
    go(cp(nblk(y, 0), nblk(y, 0), 9, sib))
    put(y, 0)
    finals = [
        pltpu.make_async_copy(masb, nm_out, lsem.at[1]),
        pltpu.make_async_copy(m1b, n1_out, lsem.at[2]),
        pltpu.make_async_copy(m2b, n2_out, lsem.at[3]),
    ]
    for c in finals:
        c.start()
    first, second = nblk(y, 1, 0), nblk(y, 1, 1)
    await_(first, 8)
    go(cp(first, first, 2, to_y[0]))
    for d in (0, 1):
        b = nblk(from_y[d], 0)
        await_(b, d)
        part = nblk(from_y[d], 0, d)
        go(cp(part, part, 4 + d, to_y[d]))
        go(cp(b, b, 11 + d, sib))
        put(from_y[d], 0)
    await_(second, 17)
    go(cp(second, second, 3, to_y[1]))
    go(cp(second, second, 18, to_y[0]))
    go(cp(first, first, 19, to_y[1]))
    for t in range(4, 8):
        hgsend(t).start()
    b = nblk(y, 1)
    go(cp(b, b, 10, sib))
    put(y, 1)
    b = nblk(y2, 0)
    for d in (0, 1):
        await_(nblk(y2, 0, d), 4 + d)
    go(cp(b, b, 15, sib))
    put(y2, 0)
    for d in (0, 1):
        part = nblk(from_y[d], 1, d)
        await_(part, 2 + d)
        go(cp(part, part, 6 + d, to_y[d]))
    for d in (0, 1):
        await_(nblk(from_y[d], 1, 1 - d), 18 + d)
        b = nblk(from_y[d], 1)
        go(cp(b, b, 13 + d, sib))
        put(from_y[d], 1)
    oc = 1 - core

    def from_sibling(yy, j, i):
        await_(nblk(yy, j, cc=oc), i)
        put(yy, j, oc)

    from_sibling(y, 0, 9)
    from_sibling(y, 1, 10)
    from_sibling(yl1, 0, 11)
    from_sibling(yr1, 0, 12)
    from_sibling(y2, 0, 15)
    b = nblk(y2, 1)
    for d in (0, 1):
        await_(nblk(y2, 1, d), 6 + d)
    go(cp(b, b, 16, sib))
    put(y2, 1)
    from_sibling(yl1, 1, 13)
    from_sibling(yr1, 1, 14)
    from_sibling(y2, 1, 16)

    got(hts, g_r)
    got(hts, lsem.at[4])
    for c in finals:
        c.wait()
    got(nwb, w_s)
    got(hts, g_s)
    got(hts, hss)
    got(cbuf.at[pl.ds(0, 7)], zs)
    got(gs.at[0, 0, pl.ds(0, 336), :], wxs)
    got(gs.at[pl.ds(0, 3), 0], wys)
    got(gs.at[:, 0], wds)
    got(gs, ds_)
    got(yfs, yf_s)
    got(yns, yn_s)
    got(xs.at[pl.ds(0, 3)], x_s)
    got(nr, n_s)
    got(nwb.at[:, pl.ds(0, 3840)], o_s)


def local(hidden, cotangent, master, moment_one, moment_two):
    dma = pltpu.SemaphoreType.DMA
    any_ = pl.BlockSpec(memory_space=pl.ANY)
    v = pltpu.VMEM
    scratch = [
        v((NK, 1024, 512), BF16),
        v((2, 2, 2, 2, FC, 512), BF16),
        v((2, FC, 1024), BF16),
        v((FC, 1024), BF16),
        v((4, 2, FC, 512), F32),
        v((4, 2, FC, 512), F32),
        v((4, 2, FC, 128), BF16),
        v((4, 2, FC, 128), BF16),
        v((4, 2, 2, FC, 128), BF16),
        v((4, 2, 2, FC, 128), BF16),
        v((4, 2, FC, 128), BF16),
        v((2, 3, FC, 128), BF16),
        v((2, FC, 128), F32),
        v((2, FC, 1024), F32),
        v((2, FC, 1024), BF16),
        v((FC, 256), F32),
        v((FC, 256), F32),
        v((FC, 256), F32),
        v((FC, 4096), BF16),
        v((2, 1, 128), F32),
        v((38, 1, 128), F32),
        dma((5,)),
        dma((NK,)),
        dma, dma((NK, 4)),
        dma, dma,
        dma, dma((2,)),
        dma, dma((2,)),
        dma, dma,
        dma, dma((4, 2)),
        dma, dma((4, 2)),
        dma, dma((4,)),
        dma, dma,
        dma, dma,
        dma, dma((2,)),
        dma, dma((20,)),
        dma,
    ]
    sds = jax.ShapeDtypeStruct
    hg, nw, nm, n1, n2 = pl.pallas_call(
        kernel,
        out_shape=(
            sds((FC, 2048), BF16),
            sds((FC, 4096), BF16),
            sds((FC, 256), F32),
            sds((FC, 256), F32),
            sds((FC, 256), F32),
        ),
        in_specs=[any_] * 5,
        out_specs=(any_,) * 5,
        scratch_shapes=scratch,
        compiler_params=pltpu.CompilerParams(
            collective_id=0, has_side_effects=True, vmem_limit_bytes=63 * 2**20
        ),
        cost_estimate=pl.CostEstimate(
            flops=15_032_385_536, bytes_accessed=16_000_000, transcendentals=0
        ),
        name="fused_backward",
    )(hidden.T, cotangent, master.T, moment_one.T, moment_two.T)
    outs = (hg, nw, nm, n1, n2)
    hg, nw, nm, n1, n2 = pl.pallas_call(
        hand_on,
        out_shape=tuple(sds(t.shape, t.dtype) for t in outs),
        in_specs=[any_] * 5,
        out_specs=(any_,) * 5,
        scratch_shapes=[v(t.shape, t.dtype) for t in outs] + [dma((2, 11))],
        compiler_params=pltpu.CompilerParams(vmem_limit_bytes=60 * 2**20),
        name="hand_on",
    )(*outs)
    return (hg.T, nw.T, nm.T, n1.T, n2.T)


def hand_on(*refs):
    srcs, dsts, bufs, sems = refs[:5], refs[5:10], refs[10:15], refs[15]
    ins, outs = [], []
    for src, dst, buf in zip(srcs, dsts, bufs):
        n = 4 if src.shape[1] > 256 else 1
        rows = FC // n
        for i in range(n):
            cut = pl.ds(i * rows, rows)
            k = len(ins)
            ins.append(pltpu.make_async_copy(src.at[cut, :], buf.at[cut, :], sems.at[0, k]))
            outs.append(pltpu.make_async_copy(buf.at[cut, :], dst.at[cut, :], sems.at[1, k]))
    for c in ins:
        c.start()
    for c, d in zip(ins, outs):
        c.wait()
        d.start()
    for d in outs:
        d.wait()


def solution(mesh):
    return jax.shard_map(
        local,
        mesh=mesh,
        in_specs=(
            P("dp", "mp"),
            P(("dp", "mp"), None),
            P("dp", "mp"),
            P("dp", "mp"),
            P("dp", "mp"),
        ),
        out_specs=(P("dp", "mp"), P(None, "mp"), P("dp", "mp"), P("dp", "mp"), P("dp", "mp")),
        check_vma=False,
    )
```

```python
import functools

import jax
import jax.numpy as jnp
from jax import lax
from jax.experimental import pallas as pl
from jax.experimental.pallas import tpu as pltpu
from jax.sharding import PartitionSpec as P

F32 = jnp.float32
BF16 = jnp.bfloat16
NT = (((1,), (1,)), ((), ()))
MESH = pl.DeviceIdType.MESH
FC = 448
NK = 8


def rem(a, n):
    return lax.rem(a, jnp.int32(n))


def div(a, n):
    return lax.div(a, jnp.int32(n))


def kernel(
    hid, cot, mas, m1, m2,
    hg_out, nw_out, nm_out, n1_out, n2_out,
    cbuf, wbuf, ht, hts, gs, gr,
    yfs, yfr, yns, ynr, xs, xr, ga, acc, hgs,
    masb, m1b, m2b, nwb, ns, nr,
    lsem, csem, zs, zr, hss, hsr, wxs, wxr, wys, wyr, wds, wdr,
    ds_, dr, yf_s, yf_r, yn_s, yn_r, x_s, x_r, g_s, g_r, n_s, n_r, o_s, o_r, w_s,
):
    dp = lax.axis_index("dp")
    mp = lax.axis_index("mp")
    core = rem(dp, 2)
    xlo = rem(div(dp, 2), 2)
    y = div(dp, 4)
    h = rem(mp, 2)
    z = div(mp, 2)
    x = h * 2 + xlo
    xr1, xl1, x2 = rem(x + 1, 4), rem(x + 3, 4), rem(x + 2, 4)
    yr1, yl1, y2 = rem(y + 1, 4), rem(y + 3, 4), rem(y + 2, 4)

    def dev(xx=x, yy=y, zz=z, cc=core):
        return ((yy * 2 + rem(xx, 2)) * 2 + cc, zz * 2 + div(xx, 2))

    def rc(src, dst, ss, rs, to):
        return pltpu.make_async_remote_copy(
            src_ref=src, dst_ref=dst, send_sem=ss, recv_sem=rs, device_id=to, device_id_type=MESH
        )

    sib = dev(cc=1 - core)

    loads = [
        pltpu.make_async_copy(mas, masb, lsem.at[0]),
        pltpu.make_async_copy(m1, m1b, lsem.at[1]),
        pltpu.make_async_copy(m2, m2b, lsem.at[2]),
    ]
    zrow = pl.multiple_of(z * 128, 128)
    for k in range(NK):
        q, p = k // 2, 1 - k % 2
        r, half = q // 2, q % 2
        xl_ = 1 - xlo if r else xlo
        c_ = 1 - core if p else core
        for yy in range(4):
            off = pl.multiple_of(((yy * 2 + xl_) * 2 + c_) * 256 + half * 128, 128)
            pltpu.make_async_copy(
                cot.at[:, pl.ds(off, 128)],
                cbuf.at[k, pl.ds(zrow, 128), pl.ds(yy * 128, 128)],
                csem.at[k],
            ).start()
        if k == 0:
            loads[0].start()
            for par, sem in ((1 - h, 3), (h, 4)):
                for t in range(8):
                    src = hid.at[:, pl.ds(pl.multiple_of((2 * t + par) * 128, 128), 128)]
                    dst = hts if sem == 3 else ht.at[h]
                    dst = dst.at[:, pl.ds(t * 128, 128)]
                    pltpu.make_async_copy(src, dst, lsem.at[sem]).start()
    loads[1].start()
    loads[2].start()

    barrier = pltpu.get_barrier_semaphore()
    peers = [sib]
    peers = [dev(xx=rem(x + i, 4), cc=1 - core if c else core) for i in range(4) for c in (0, 1) if i + c]
    peers += [dev(yy=rem(y + i, 4)) for i in range(1, 4)]
    peers += [dev(zz=rem(z + i, 8)) for i in range(1, 8)]
    for to in peers:
        pl.semaphore_signal(barrier, inc=1, device_id=to, device_id_type=MESH)
    pl.semaphore_wait(barrier, len(peers))

    zto = (dev(zz=rem(z + 1, 8)), dev(zz=rem(z + 7, 8)))

    def zcopy(d, k, hop):
        slot = rem(z + 16 - hop, 8) if d == 0 else rem(z + hop, 8)
        row, n = slot * 128, 128
        if hop == 3:
            n = 64
            row = row + 64 * d
        ref = cbuf.at[k, pl.ds(pl.multiple_of(row, 64), n), :]
        return rc(ref, ref, zs, zr.at[k, hop], zto[d])

    def zown(k):
        own = cbuf.at[k, pl.ds(zrow, 128), :]
        pltpu.make_async_copy(own, own, csem.at[k]).wait()
        for d in (0, 1):
            zcopy(d, k, 0).start()

    def got(ref, sem):
        pltpu.make_async_copy(ref, ref, sem).wait()

    def zwait(k, hop):
        got(cbuf.at[k, pl.ds(0, 256 if hop < 3 else 128), :], zr.at[k, hop])

    def zring(s):
        def forward(k, hop):
            zwait(k, hop - 1)
            for d in (0, 1):
                zcopy(d, k, hop).start()

        for hop in (3, 2, 1):

            @pl.when((s >= hop) & (s - hop < NK - 1))
            def _(hop=hop):
                forward(s - hop, hop)

            @pl.when(s - hop == NK - 2)
            def _(hop=hop):
                forward(jnp.int32(NK - 1), hop)

        @pl.when(s < NK - 1)
        def _():
            zown(s + 1)

    def wblk(xx, yy, p, rows=None):
        lanes = pl.ds(pl.multiple_of(yy * 128, 128), 128)
        r_ = slice(None) if rows is None else pl.ds(rows[0], rows[1])
        return wbuf.at[rem(xx, 2), :, p, div(xx, 2), r_, lanes]

    def wx(d, far):
        src = x if not far else (xl1 if d == 0 else xr1)
        blk = wblk(src, y, 0, (d * 224, 224) if far else None)
        return rc(blk, blk, wxs, wxr.at[far], dev(xx=xr1 if d == 0 else xl1))

    def wy(j, d, far):
        src = y if not far else (yl1 if d == 0 else yr1)
        blk = wblk(rem(x + j, 4), src, 0, (d * 224, 224) if far else None)
        return rc(blk, blk, wys, wyr.at[far], dev(yy=yr1 if d == 0 else yl1))

    def wd(j):
        xx = rem(x + j, 4)
        src = wbuf.at[rem(xx, 2), :, 0, div(xx, 2), :, :]
        dst = wbuf.at[rem(xx, 2), :, 1, div(xx, 2), :, :]
        return rc(src, dst, wds, wdr, sib)

    def hsend(d):
        rows = pl.ds(d * 224, 224)
        dst = ht.at[h, rows, :]
        return rc(hts.at[rows, :], dst, hss, hsr, dev(xx=x2))

    def gd(q, f):
        return rc(gs.at[q, f], gr.at[q, f], ds_, dr.at[q, f], sib)

    def gyfar(q, f):
        return rc(
            yfs.at[q, f], yfr.at[q, f], yf_s, yf_r.at[q, f], dev(yy=yr1 if f == 0 else yl1)
        )

    def gynear(q, d, f):
        return rc(
            yns.at[q, d, f], ynr.at[q, d, f], yn_s, yn_r.at[q],
            dev(yy=yr1 if d == 0 else yl1),
        )

    def lanes(yy):
        return pl.ds(pl.multiple_of(yy * 128, 128), 128)

    def gradient_chunk(kc):
        q = div(kc, 2)
        part = kc - 2 * q
        zwait(kc, 3)

        @pl.when(part == 0)
        def _():
            def body(f, c):
                gs[q, f] = jnp.dot(ht[f], cbuf[kc], preferred_element_type=F32)
                gd(q, f).start()
                return c

            lax.fori_loop(0, 2, body, 0)

        @pl.when(part == 1)
        def _():
            for f in (0, 1):
                own = jnp.dot(ht[f], cbuf[kc], preferred_element_type=F32)
                gd(q, f).wait_recv()
                gr[q, f] = gr[q, f] + own
                yfs[q, f] = gr[q, f, :, lanes(y2)].astype(BF16)
                gyfar(q, f).start()
            for f in (1, 0):
                yns[q, 1 - f, f] = gr[q, f, :, lanes(yl1 if f == 0 else yr1)].astype(BF16)
                gynear(q, 1 - f, f).start()

    def ystep2(q):
        for f in (0, 1):
            gyfar(q, f).wait_recv()
            own = gr[q, f, :, lanes(yr1 if f == 0 else yl1)]
            yns[q, f, f] = (own + yfr[q, f].astype(F32)).astype(BF16)
            gynear(q, f, f).start()

    def xsend(q, i):
        half = q % 2
        if q < 2:
            return rc(xs.at[q, 0], xr.at[half, 2], x_s, x_r, dev(xx=x2))
        return rc(xs.at[q, i], xr.at[half, h], x_s, x_r, dev(xx=i * 2 + 1 - xlo))

    def ystep3(q):
        got(ynr.at[q], yn_r.at[q])

        def total(f):
            return (
                gr[q, f, :, lanes(y)] + ynr[q, 0, f].astype(F32) + ynr[q, 1, f].astype(F32)
            )

        if q < 2:
            ga[q] = total(h)
            xs[q, 0] = total(1 - h).astype(BF16)
            xsend(q, 0).start()
        else:
            for f in (0, 1):
                xs[q, f] = total(f).astype(BF16)
                xsend(q, f).start()

    def hg_tile(k, f, toks):
        u = div(k, 2)
        r, half, p = div(u, 2), rem(u, 2), 1 - rem(k, 2)
        w = wbuf[xlo + r - 2 * xlo * r, half, p, f]
        return lax.dot_general(w, cbuf[k, toks, :], NT, preferred_element_type=F32)

    def tile(i):
        return div(i, 4), pl.ds(pl.multiple_of(rem(i, 4) * 256, 256), 256)

    def hg_first():
        def body(i, c):
            f, toks = tile(i)
            acc[f, :, toks] = hg_tile(0, f, toks) + hg_tile(1, f, toks)
            return c

        lax.fori_loop(0, 8, body, 0)

    def hg_add(k):
        k = jnp.int32(k)

        def body(i, c):
            f, toks = tile(i)
            acc[f, :, toks] = acc[f, :, toks] + hg_tile(k, f, toks) + hg_tile(k + 1, f, toks)
            return c

        lax.fori_loop(0, 8, body, 0)

    def hg_one(k):
        def body(i, c):
            f, toks = tile(i)
            acc[f, :, toks] = acc[f, :, toks] + hg_tile(k, f, toks)
            return c

        lax.fori_loop(0, 8, body, 0)

    def hg_last(f):
        def body(i, c):
            toks = tile(i)[1]
            a = hg_tile(jnp.int32(5), f, toks) + hg_tile(jnp.int32(6), f, toks)
            a += hg_tile(jnp.int32(7), f, toks)
            hgs[f, :, toks] = (acc[f, :, toks] + a).astype(BF16)
            return c

        lax.fori_loop(0, 4, body, 0)

    def hgout(t, par):
        return hg_out.at[:, pl.ds(pl.multiple_of((2 * t + par) * 128, 128), 128)]

    def hgsend(t):
        src = hgs.at[1 - h, :, pl.ds(t * 128, 128)]
        dst = hgout(t, h)
        return rc(src, dst, g_s, g_r, dev(xx=x2))

    def own_hg_copy():
        for t in range(8):
            src = hgs.at[h, :, pl.ds(t * 128, 128)]
            pltpu.make_async_copy(src, hgout(t, h), lsem.at[4]).start()

    zown(jnp.int32(0))
    zown(jnp.int32(1))
    loads[0].wait()
    for half in (0, 1):
        wbuf[xlo, half, 0, h, :, lanes(y)] = masb[:, half * 128 : half * 128 + 128].astype(BF16)
    wx(0, 0).start()
    wx(1, 0).start()
    wy(0, 0, 0).start()
    wy(0, 1, 0).start()
    pltpu.make_async_copy(hts, ht.at[h], lsem.at[4]).wait()

    def tick(s, c):
        @pl.when(s >= 6)
        def _():
            gradient_chunk(s - 4)

        zring(s)

        @pl.when(s == 1)
        def _():
            got(gs.at[0, 0, pl.ds(0, 224), :], wxr.at[0])
            for d in (0, 1):
                wx(d, 1).start()
            for j in (1, 3):
                for d in (0, 1):
                    wy(j, d, 0).start()

        @pl.when(s == 2)
        def _():
            got(gs.at[0, 0, pl.ds(0, 112), :], wxr.at[1])
            for d in (0, 1):
                wy(2, d, 0).start()
            pltpu.make_async_copy(hts, hts, lsem.at[3]).wait()
            for d in (0, 1):
                hsend(d).start()

        @pl.when(s == 4)
        def _():
            got(gs.at[0], wyr.at[0])
            for j in range(4):
                for d in (0, 1):
                    wy(j, d, 1).start()

        @pl.when(s == 5)
        def _():
            got(hts, hsr)
            gradient_chunk(jnp.int32(0))
            got(gs.at[0, 0], wyr.at[1])
            for j in range(4):
                wd(j).start()

        @pl.when(s == 6)
        def _():
            gradient_chunk(jnp.int32(1))

        for q in range(2):

            @pl.when(s == (7, 8)[q])
            def _(q=q):
                ystep2(q)

        for q in range(2):

            @pl.when(s == (8, 9)[q])
            def _(q=q):
                ystep3(q)

        @pl.when(s == 6)
        def _():
            got(gs.at[:, 0], wdr)
            hg_first()

        @pl.when(s == 7)
        def _():
            hg_add(2)

        @pl.when(s == 8)
        def _():
            hg_one(jnp.int32(4))

        return c

    lax.fori_loop(1, 11, tick, 0)

    ystep2(2)
    gradient_chunk(jnp.int32(7))
    hg_last(1 - h)
    ystep3(2)
    for t in range(2):
        hgsend(t).start()
    ystep2(3)
    hg_last(h)
    own_hg_copy()
    ystep3(3)
    loads[1].wait()
    loads[2].wait()
    sq = jnp.zeros((8, 128), F32)
    got(xr, x_r)
    for half in (0, 1):
        g = (
            ga[half]
            + xr[half, 2].astype(F32)
            + xr[half, 0].astype(F32)
            + xr[half, 1].astype(F32)
        )
        ga[half] = g
        sq = sq + jnp.sum((g * g).reshape(FC // 8, 8, 128), axis=0)

    groups = [
        [dev(xx=rem(x + i, 4), cc=1 - core if c else core) for i in range(4) for c in (0, 1) if i + c],
        [dev(yy=rem(y + i, 4)) for i in range(1, 4)],
        [dev(zz=rem(z + i, 8)) for i in range(1, 8)],
    ]
    base = 0
    for ph, group in enumerate(groups):
        ns[ph] = jnp.sum(sq, axis=0, keepdims=True)
        for i, to in enumerate(group):
            rc(ns.at[ph], nr.at[base + i], n_s, n_r.at[ph], to).start()
        if ph == 2:
            for t in range(2, 4):
                hgsend(t).start()
        heard = nr.at[pl.ds(base, len(group))]
        got(heard, n_r.at[ph])
        sq = ns[ph] + jnp.sum(heard[...], axis=0)
        base += len(group)
    squares = jnp.sum(sq, keepdims=True)
    scale = jnp.minimum(1.0, 1.0 / (jnp.sqrt(squares) + 1e-06))

    for half in (0, 1):
        cols = pl.ds(half * 128, 128)
        clipped = scale * ga[half]
        nm1 = 0.9 * m1b[:, cols] + 0.1 * clipped
        nm2 = 0.95 * m2b[:, cols] + 0.05 * clipped * clipped
        first_hat = nm1 / (1.0 - 0.9**10)
        second_hat = nm2 / (1.0 - 0.95**10)
        w = masb[:, cols]
        nmas = w - 0.01 * (first_hat / (jnp.sqrt(second_hat) + 1e-08) + 0.1 * w)
        m1b[:, cols] = nm1
        m2b[:, cols] = nm2
        masb[:, cols] = nmas
        nwb[:, pl.ds(pl.multiple_of(dp * 256 + half * 128, 128), 128)] = nmas.astype(BF16)

    def nblk(yy, j, half=None, cc=core):
        xl_ = 1 - xlo if j else xlo
        off = ((yy * 2 + xl_) * 2 + cc) * 256
        rows = slice(None) if half is None else pl.ds(half * 224, 224)
        return nwb.at[rows, pl.ds(pl.multiple_of(off, 256), 256)]

    def cp(src, dst, i, to):
        return rc(src, dst, o_s, o_r.at[i], to)

    to_y = (dev(yy=yr1), dev(yy=yl1))
    from_y = (yl1, yr1)
    to_x = dev(xx=h * 2 + 1 - xlo)

    def go(c):
        c.start()

    def put(yy, j, cc=core):
        off = pl.multiple_of(((yy * 2 + (1 - xlo if j else xlo)) * 2 + cc) * 256, 256)
        c = pltpu.make_async_copy(
            nblk(yy, j, cc=cc), nw_out.at[:, pl.ds(off, 256)], w_s
        )
        c.start()

    def await_(blk, i):
        cp(blk, blk, i, sib).wait_recv()

    for i in (0, 1):
        go(cp(nblk(y, 0, i), nblk(y, 0, i), 8 + 9 * i, to_x))
    for d in (0, 1):
        go(cp(nblk(y, 0), nblk(y, 0), d, to_y[d]))
    go(cp(nblk(y, 0), nblk(y, 0), 9, sib))
    put(y, 0)
    finals = [
        pltpu.make_async_copy(masb, nm_out, lsem.at[1]),
        pltpu.make_async_copy(m1b, n1_out, lsem.at[2]),
        pltpu.make_async_copy(m2b, n2_out, lsem.at[3]),
    ]
    for c in finals:
        c.start()
    first, second = nblk(y, 1, 0), nblk(y, 1, 1)
    await_(first, 8)
    go(cp(first, first, 2, to_y[0]))
    for d in (0, 1):
        b = nblk(from_y[d], 0)
        await_(b, d)
        part = nblk(from_y[d], 0, d)
        go(cp(part, part, 4 + d, to_y[d]))
        go(cp(b, b, 11 + d, sib))
        put(from_y[d], 0)
    await_(second, 17)
    go(cp(second, second, 3, to_y[1]))
    go(cp(second, second, 18, to_y[0]))
    go(cp(first, first, 19, to_y[1]))
    for t in range(4, 8):
        hgsend(t).start()
    b = nblk(y, 1)
    go(cp(b, b, 10, sib))
    put(y, 1)
    b = nblk(y2, 0)
    for d in (0, 1):
        await_(nblk(y2, 0, d), 4 + d)
    go(cp(b, b, 15, sib))
    put(y2, 0)
    for d in (0, 1):
        part = nblk(from_y[d], 1, d)
        await_(part, 2 + d)
        go(cp(part, part, 6 + d, to_y[d]))
    for d in (0, 1):
        await_(nblk(from_y[d], 1, 1 - d), 18 + d)
        b = nblk(from_y[d], 1)
        go(cp(b, b, 13 + d, sib))
        put(from_y[d], 1)
    oc = 1 - core

    def from_sibling(yy, j, i):
        await_(nblk(yy, j, cc=oc), i)
        put(yy, j, oc)

    from_sibling(y, 0, 9)
    from_sibling(y, 1, 10)
    from_sibling(yl1, 0, 11)
    from_sibling(yr1, 0, 12)
    from_sibling(y2, 0, 15)
    b = nblk(y2, 1)
    for d in (0, 1):
        await_(nblk(y2, 1, d), 6 + d)
    go(cp(b, b, 16, sib))
    put(y2, 1)
    from_sibling(yl1, 1, 13)
    from_sibling(yr1, 1, 14)
    from_sibling(y2, 1, 16)

    got(hts, g_r)
    got(hts, lsem.at[4])
    for c in finals:
        c.wait()
    got(nwb, w_s)
    got(hts, g_s)
    got(hts, hss)
    got(cbuf.at[pl.ds(0, 7)], zs)
    got(gs.at[0, 0, pl.ds(0, 336), :], wxs)
    got(gs.at[pl.ds(0, 3), 0], wys)
    got(gs.at[:, 0], wds)
    got(gs, ds_)
    got(yfs, yf_s)
    got(yns, yn_s)
    got(xs.at[pl.ds(0, 3)], x_s)
    got(nr, n_s)
    got(nwb.at[:, pl.ds(0, 3840)], o_s)


def local(hidden, cotangent, master, moment_one, moment_two):
    dma = pltpu.SemaphoreType.DMA
    any_ = pl.BlockSpec(memory_space=pl.ANY)
    v = pltpu.VMEM
    scratch = [
        v((NK, 1024, 512), BF16),
        v((2, 2, 2, 2, FC, 512), BF16),
        v((2, FC, 1024), BF16),
        v((FC, 1024), BF16),
        v((4, 2, FC, 512), F32),
        v((4, 2, FC, 512), F32),
        v((4, 2, FC, 128), BF16),
        v((4, 2, FC, 128), BF16),
        v((4, 2, 2, FC, 128), BF16),
        v((4, 2, 2, FC, 128), BF16),
        v((4, 2, FC, 128), BF16),
        v((2, 3, FC, 128), BF16),
        v((2, FC, 128), F32),
        v((2, FC, 1024), F32),
        v((2, FC, 1024), BF16),
        v((FC, 256), F32),
        v((FC, 256), F32),
        v((FC, 256), F32),
        v((FC, 4096), BF16),
        v((3, 1, 128), F32),
        v((17, 1, 128), F32),
        dma((5,)),
        dma((NK,)),
        dma, dma((NK, 4)),
        dma, dma,
        dma, dma((2,)),
        dma, dma((2,)),
        dma, dma,
        dma, dma((4, 2)),
        dma, dma((4, 2)),
        dma, dma((4,)),
        dma, dma,
        dma, dma,
        dma, dma((3,)),
        dma, dma((20,)),
        dma,
    ]
    sds = jax.ShapeDtypeStruct
    hg, nw, nm, n1, n2 = pl.pallas_call(
        kernel,
        out_shape=(
            sds((FC, 2048), BF16),
            sds((FC, 4096), BF16),
            sds((FC, 256), F32),
            sds((FC, 256), F32),
            sds((FC, 256), F32),
        ),
        in_specs=[any_] * 5,
        out_specs=(any_,) * 5,
        scratch_shapes=scratch,
        compiler_params=pltpu.CompilerParams(
            collective_id=0, has_side_effects=True, vmem_limit_bytes=63 * 2**20
        ),
        cost_estimate=pl.CostEstimate(
            flops=15_032_385_536, bytes_accessed=16_000_000, transcendentals=0
        ),
        name="fused_backward",
    )(hidden.T, cotangent, master.T, moment_one.T, moment_two.T)
    outs = (hg, nw, nm, n1, n2)
    hg, nw, nm, n1, n2 = pl.pallas_call(
        hand_on,
        out_shape=tuple(sds(t.shape, t.dtype) for t in outs),
        in_specs=[any_] * 5,
        out_specs=(any_,) * 5,
        scratch_shapes=[v(t.shape, t.dtype) for t in outs] + [dma((2, 11))],
        compiler_params=pltpu.CompilerParams(vmem_limit_bytes=60 * 2**20),
        name="hand_on",
    )(*outs)
    return (hg.T, nw.T, nm.T, n1.T, n2.T)


def hand_on(*refs):
    srcs, dsts, bufs, sems = refs[:5], refs[5:10], refs[10:15], refs[15]
    ins, outs = [], []
    for src, dst, buf in zip(srcs, dsts, bufs):
        n = 4 if src.shape[1] > 256 else 1
        rows = FC // n
        for i in range(n):
            cut = pl.ds(i * rows, rows)
            k = len(ins)
            ins.append(pltpu.make_async_copy(src.at[cut, :], buf.at[cut, :], sems.at[0, k]))
            outs.append(pltpu.make_async_copy(buf.at[cut, :], dst.at[cut, :], sems.at[1, k]))
    for c in ins:
        c.start()
    for c, d in zip(ins, outs):
        c.wait()
        d.start()
    for d in outs:
        d.wait()


def solution(mesh):
    return jax.shard_map(
        local,
        mesh=mesh,
        in_specs=(
            P("dp", "mp"),
            P(("dp", "mp"), None),
            P("dp", "mp"),
            P("dp", "mp"),
            P("dp", "mp"),
        ),
        out_specs=(P("dp", "mp"), P(None, "mp"), P("dp", "mp"), P("dp", "mp"), P("dp", "mp")),
        check_vma=False,
    )
```

```python
import functools

import jax
import jax.numpy as jnp
from jax import lax
from jax.experimental import pallas as pl
from jax.experimental.pallas import tpu as pltpu
from jax.sharding import PartitionSpec as P

F32 = jnp.float32
BF16 = jnp.bfloat16
NT = (((1,), (1,)), ((), ()))
MESH = pl.DeviceIdType.MESH
FC = 448
NK = 8


def rem(a, n):
    return lax.rem(a, jnp.int32(n))


def div(a, n):
    return lax.div(a, jnp.int32(n))


def kernel(
    hid, cot, mas, m1, m2,
    hg_out, nw_out, nm_out, n1_out, n2_out,
    cbuf, wbuf, ht, hts, gs, gr,
    yfs, yfr, yns, ynr, xs, xr, ga, acc, hgs,
    masb, m1b, m2b, nwb, ns, nr,
    lsem, csem, zs, zr, hss, hsr, wxs, wxr, wys, wyr, wds, wdr,
    ds_, dr, yf_s, yf_r, yn_s, yn_r, x_s, x_r, g_s, g_r, n_s, n_r, o_s, o_r, w_s,
):
    dp = lax.axis_index("dp")
    mp = lax.axis_index("mp")
    core = rem(dp, 2)
    xlo = rem(div(dp, 2), 2)
    y = div(dp, 4)
    h = rem(mp, 2)
    z = div(mp, 2)
    x = h * 2 + xlo
    xr1, xl1, x2 = rem(x + 1, 4), rem(x + 3, 4), rem(x + 2, 4)
    yr1, yl1, y2 = rem(y + 1, 4), rem(y + 3, 4), rem(y + 2, 4)

    def dev(xx=x, yy=y, zz=z, cc=core):
        return ((yy * 2 + rem(xx, 2)) * 2 + cc, zz * 2 + div(xx, 2))

    def rc(src, dst, ss, rs, to):
        return pltpu.make_async_remote_copy(
            src_ref=src, dst_ref=dst, send_sem=ss, recv_sem=rs, device_id=to, device_id_type=MESH
        )

    sib = dev(cc=1 - core)

    loads = [
        pltpu.make_async_copy(mas, masb, lsem.at[0]),
        pltpu.make_async_copy(m1, m1b, lsem.at[1]),
        pltpu.make_async_copy(m2, m2b, lsem.at[2]),
    ]
    zrow = pl.multiple_of(z * 128, 128)
    for k in range(NK):
        q, p = k // 2, 1 - k % 2
        r, half = q // 2, q % 2
        xl_ = 1 - xlo if r else xlo
        c_ = 1 - core if p else core
        for yy in range(4):
            off = pl.multiple_of(((yy * 2 + xl_) * 2 + c_) * 256 + half * 128, 128)
            pltpu.make_async_copy(
                cot.at[:, pl.ds(off, 128)],
                cbuf.at[k, pl.ds(zrow, 128), pl.ds(yy * 128, 128)],
                csem.at[k],
            ).start()
        if k == 0:
            loads[0].start()
            for par, sem in ((1 - h, 3), (h, 4)):
                for t in range(8):
                    src = hid.at[:, pl.ds(pl.multiple_of((2 * t + par) * 128, 128), 128)]
                    dst = hts if sem == 3 else ht.at[h]
                    dst = dst.at[:, pl.ds(t * 128, 128)]
                    pltpu.make_async_copy(src, dst, lsem.at[sem]).start()
    loads[1].start()
    loads[2].start()

    barrier = pltpu.get_barrier_semaphore()
    peers = [sib]
    peers = [dev(xx=rem(x + i, 4), cc=1 - core if c else core) for i in range(4) for c in (0, 1) if i + c]
    peers += [dev(yy=rem(y + i, 4)) for i in range(1, 4)]
    peers += [dev(zz=rem(z + i, 8)) for i in range(1, 8)]
    for to in peers:
        pl.semaphore_signal(barrier, inc=1, device_id=to, device_id_type=MESH)
    pl.semaphore_wait(barrier, len(peers))

    zto = (dev(zz=rem(z + 1, 8)), dev(zz=rem(z + 7, 8)))

    def zcopy(d, k, hop):
        slot = rem(z + 16 - hop, 8) if d == 0 else rem(z + hop, 8)
        row, n = slot * 128, 128
        if hop == 3:
            n = 64
            row = row + 64 * d
        ref = cbuf.at[k, pl.ds(pl.multiple_of(row, 64), n), :]
        return rc(ref, ref, zs, zr.at[k, hop], zto[d])

    def zown(k):
        own = cbuf.at[k, pl.ds(zrow, 128), :]
        pltpu.make_async_copy(own, own, csem.at[k]).wait()
        for d in (0, 1):
            zcopy(d, k, 0).start()

    def got(ref, sem):
        pltpu.make_async_copy(ref, ref, sem).wait()

    def zwait(k, hop):
        got(cbuf.at[k, pl.ds(0, 256 if hop < 3 else 128), :], zr.at[k, hop])

    def zring(s):
        def forward(k, hop):
            zwait(k, hop - 1)
            for d in (0, 1):
                zcopy(d, k, hop).start()

        for hop in (3, 2, 1):

            @pl.when((s >= hop) & (s - hop < NK - 1))
            def _(hop=hop):
                forward(s - hop, hop)

            @pl.when(s - hop == NK - 2)
            def _(hop=hop):
                forward(jnp.int32(NK - 1), hop)

        @pl.when(s < NK - 1)
        def _():
            zown(s + 1)

    def wblk(xx, yy, p, rows=None):
        lanes = pl.ds(pl.multiple_of(yy * 128, 128), 128)
        r_ = slice(None) if rows is None else pl.ds(rows[0], rows[1])
        return wbuf.at[rem(xx, 2), :, p, div(xx, 2), r_, lanes]

    def wx(d, far):
        src = x if not far else (xl1 if d == 0 else xr1)
        blk = wblk(src, y, 0, (d * 224, 224) if far else None)
        return rc(blk, blk, wxs, wxr.at[far], dev(xx=xr1 if d == 0 else xl1))

    def wy(j, d, far):
        src = y if not far else (yl1 if d == 0 else yr1)
        blk = wblk(rem(x + j, 4), src, 0, (d * 224, 224) if far else None)
        return rc(blk, blk, wys, wyr.at[far], dev(yy=yr1 if d == 0 else yl1))

    def wd(j):
        xx = rem(x + j, 4)
        src = wbuf.at[rem(xx, 2), :, 0, div(xx, 2), :, :]
        dst = wbuf.at[rem(xx, 2), :, 1, div(xx, 2), :, :]
        return rc(src, dst, wds, wdr, sib)

    def hsend(d):
        rows = pl.ds(d * 224, 224)
        dst = ht.at[h, rows, :]
        return rc(hts.at[rows, :], dst, hss, hsr, dev(xx=x2))

    def gd(q, f):
        return rc(gs.at[q, f], gr.at[q, f], ds_, dr.at[q, f], sib)

    def gyfar(q, f):
        return rc(
            yfs.at[q, f], yfr.at[q, f], yf_s, yf_r.at[q, f], dev(yy=yr1 if f == 0 else yl1)
        )

    def gynear(q, d, f):
        return rc(
            yns.at[q, d, f], ynr.at[q, d, f], yn_s, yn_r.at[q],
            dev(yy=yr1 if d == 0 else yl1),
        )

    def lanes(yy):
        return pl.ds(pl.multiple_of(yy * 128, 128), 128)

    def gradient_chunk(kc):
        q = div(kc, 2)
        part = kc - 2 * q
        zwait(kc, 3)

        @pl.when(part == 0)
        def _():
            def body(f, c):
                gs[q, f] = jnp.dot(ht[f], cbuf[kc], preferred_element_type=F32)
                gd(q, f).start()
                return c

            lax.fori_loop(0, 2, body, 0)

        @pl.when(part == 1)
        def _():
            for f in (0, 1):
                own = jnp.dot(ht[f], cbuf[kc], preferred_element_type=F32)
                gd(q, f).wait_recv()
                gr[q, f] = gr[q, f] + own
                yfs[q, f] = gr[q, f, :, lanes(y2)].astype(BF16)
                gyfar(q, f).start()
            for f in (1, 0):
                yns[q, 1 - f, f] = gr[q, f, :, lanes(yl1 if f == 0 else yr1)].astype(BF16)
                gynear(q, 1 - f, f).start()

    def ystep2(q):
        for f in (0, 1):
            gyfar(q, f).wait_recv()
            own = gr[q, f, :, lanes(yr1 if f == 0 else yl1)]
            yns[q, f, f] = (own + yfr[q, f].astype(F32)).astype(BF16)
            gynear(q, f, f).start()

    def xsend(q, i):
        half = q % 2
        if q < 2:
            return rc(xs.at[q, 0], xr.at[half, 2], x_s, x_r, dev(xx=x2))
        return rc(xs.at[q, i], xr.at[half, h], x_s, x_r, dev(xx=i * 2 + 1 - xlo))

    def ystep3(q):
        got(ynr.at[q], yn_r.at[q])

        def total(f):
            return (
                gr[q, f, :, lanes(y)] + ynr[q, 0, f].astype(F32) + ynr[q, 1, f].astype(F32)
            )

        if q < 2:
            ga[q] = total(h)
            xs[q, 0] = total(1 - h).astype(BF16)
            xsend(q, 0).start()
        else:
            for f in (0, 1):
                xs[q, f] = total(f).astype(BF16)
                xsend(q, f).start()

    def hg_tile(k, f, toks):
        u = div(k, 2)
        r, half, p = div(u, 2), rem(u, 2), 1 - rem(k, 2)
        w = wbuf[xlo + r - 2 * xlo * r, half, p, f]
        return lax.dot_general(w, cbuf[k, toks, :], NT, preferred_element_type=F32)

    def tile(i):
        return div(i, 4), pl.ds(pl.multiple_of(rem(i, 4) * 256, 256), 256)

    def hg_first():
        def body(i, c):
            f, toks = tile(i)
            acc[f, :, toks] = hg_tile(0, f, toks) + hg_tile(1, f, toks)
            return c

        lax.fori_loop(0, 8, body, 0)

    def hg_add(k):
        k = jnp.int32(k)

        def body(i, c):
            f, toks = tile(i)
            acc[f, :, toks] = acc[f, :, toks] + hg_tile(k, f, toks) + hg_tile(k + 1, f, toks)
            return c

        lax.fori_loop(0, 8, body, 0)

    def hg_one(k):
        def body(i, c):
            f, toks = tile(i)
            acc[f, :, toks] = acc[f, :, toks] + hg_tile(k, f, toks)
            return c

        lax.fori_loop(0, 8, body, 0)

    def hg_last(f):
        def body(i, c):
            toks = tile(i)[1]
            a = hg_tile(jnp.int32(5), f, toks) + hg_tile(jnp.int32(6), f, toks)
            a += hg_tile(jnp.int32(7), f, toks)
            hgs[f, :, toks] = (acc[f, :, toks] + a).astype(BF16)
            return c

        lax.fori_loop(0, 4, body, 0)

    def hgout(t, par):
        return hg_out.at[:, pl.ds(pl.multiple_of((2 * t + par) * 128, 128), 128)]

    def hgsend(t):
        src = hgs.at[1 - h, :, pl.ds(t * 128, 128)]
        dst = hgout(t, h)
        return rc(src, dst, g_s, g_r, dev(xx=x2))

    def own_hg_copy():
        for t in range(8):
            src = hgs.at[h, :, pl.ds(t * 128, 128)]
            pltpu.make_async_copy(src, hgout(t, h), lsem.at[4]).start()

    zown(jnp.int32(0))
    zown(jnp.int32(1))
    loads[0].wait()
    for half in (0, 1):
        wbuf[xlo, half, 0, h, :, lanes(y)] = masb[:, half * 128 : half * 128 + 128].astype(BF16)
    wx(0, 0).start()
    wx(1, 0).start()
    wy(0, 0, 0).start()
    wy(0, 1, 0).start()
    pltpu.make_async_copy(hts, ht.at[h], lsem.at[4]).wait()

    def tick(s, c):
        @pl.when(s >= 6)
        def _():
            gradient_chunk(s - 4)

        zring(s)

        @pl.when(s == 1)
        def _():
            got(gs.at[0, 0, pl.ds(0, 224), :], wxr.at[0])
            for d in (0, 1):
                wx(d, 1).start()
            for j in (1, 3):
                for d in (0, 1):
                    wy(j, d, 0).start()

        @pl.when(s == 2)
        def _():
            got(gs.at[0, 0, pl.ds(0, 112), :], wxr.at[1])
            for d in (0, 1):
                wy(2, d, 0).start()
            pltpu.make_async_copy(hts, hts, lsem.at[3]).wait()
            for d in (0, 1):
                hsend(d).start()

        @pl.when(s == 4)
        def _():
            got(gs.at[0], wyr.at[0])
            for j in range(4):
                for d in (0, 1):
                    wy(j, d, 1).start()

        @pl.when(s == 5)
        def _():
            got(hts, hsr)
            gradient_chunk(jnp.int32(0))
            got(gs.at[0, 0], wyr.at[1])
            for j in range(4):
                wd(j).start()

        @pl.when(s == 6)
        def _():
            gradient_chunk(jnp.int32(1))

        for q in range(2):

            @pl.when(s == (7, 8)[q])
            def _(q=q):
                ystep2(q)

        for q in range(2):

            @pl.when(s == (8, 9)[q])
            def _(q=q):
                ystep3(q)

        @pl.when(s == 6)
        def _():
            got(gs.at[:, 0], wdr)
            hg_first()

        @pl.when(s == 7)
        def _():
            hg_add(2)

        @pl.when(s == 8)
        def _():
            hg_one(jnp.int32(4))

        return c

    lax.fori_loop(1, 11, tick, 0)

    ystep2(2)
    gradient_chunk(jnp.int32(7))
    hg_last(1 - h)
    ystep3(2)
    for t in range(2):
        hgsend(t).start()
    ystep2(3)
    hg_last(h)
    own_hg_copy()
    ystep3(3)
    loads[1].wait()
    loads[2].wait()
    sq = jnp.zeros((8, 128), F32)
    got(xr, x_r)
    for half in (0, 1):
        g = (
            ga[half]
            + xr[half, 2].astype(F32)
            + xr[half, 0].astype(F32)
            + xr[half, 1].astype(F32)
        )
        ga[half] = g
        sq = sq + jnp.sum((g * g).reshape(FC // 8, 8, 128), axis=0)

    groups = [
        [dev(xx=rem(x + i, 4), cc=1 - core if c else core) for i in range(4) for c in (0, 1) if i + c],
        [dev(yy=rem(y + i, 4)) for i in range(1, 4)],
        [dev(zz=rem(z + i, 8)) for i in range(1, 8)],
    ]
    base = 0
    for ph, group in enumerate(groups):
        ns[ph] = jnp.sum(sq, axis=0, keepdims=True)
        for i, to in enumerate(group):
            rc(ns.at[ph], nr.at[base + i], n_s, n_r.at[ph], to).start()
        if ph == 2:
            for t in range(2, 4):
                hgsend(t).start()
        heard = nr.at[pl.ds(base, len(group))]
        got(heard, n_r.at[ph])
        sq = ns[ph] + jnp.sum(heard[...], axis=0)
        base += len(group)
    squares = jnp.sum(sq, keepdims=True)
    scale = jnp.minimum(1.0, 1.0 / (jnp.sqrt(squares) + 1e-06))

    for half in (0, 1):
        cols = pl.ds(half * 128, 128)
        clipped = scale * ga[half]
        nm1 = 0.9 * m1b[:, cols] + 0.1 * clipped
        nm2 = 0.95 * m2b[:, cols] + 0.05 * clipped * clipped
        first_hat = nm1 / (1.0 - 0.9**10)
        second_hat = nm2 / (1.0 - 0.95**10)
        w = masb[:, cols]
        nmas = w - 0.01 * (first_hat / (jnp.sqrt(second_hat) + 1e-08) + 0.1 * w)
        m1b[:, cols] = nm1
        m2b[:, cols] = nm2
        masb[:, cols] = nmas
        nwb[:, pl.ds(pl.multiple_of(dp * 256 + half * 128, 128), 128)] = nmas.astype(BF16)

    def nblk(yy, j, half=None, cc=core):
        xl_ = 1 - xlo if j else xlo
        off = ((yy * 2 + xl_) * 2 + cc) * 256
        rows = slice(None) if half is None else pl.ds(half * 224, 224)
        return nwb.at[rows, pl.ds(pl.multiple_of(off, 256), 256)]

    def cp(src, dst, i, to):
        return rc(src, dst, o_s, o_r.at[i], to)

    to_y = (dev(yy=yr1), dev(yy=yl1))
    from_y = (yl1, yr1)
    to_x = dev(xx=h * 2 + 1 - xlo)

    def go(c):
        c.start()

    def put(yy, j, cc=core):
        off = pl.multiple_of(((yy * 2 + (1 - xlo if j else xlo)) * 2 + cc) * 256, 256)
        c = pltpu.make_async_copy(
            nblk(yy, j, cc=cc), nw_out.at[:, pl.ds(off, 256)], w_s
        )
        c.start()

    def await_(blk, i):
        cp(blk, blk, i, sib).wait_recv()

    for i in (0, 1):
        go(cp(nblk(y, 0, i), nblk(y, 0, i), 8 + 9 * i, to_x))
    for i in (0, 1):
        for d in (0, 1):
            part = nblk(y, 0, d if i == 0 else 1 - d)
            go(cp(part, part, d + 20 * i, to_y[d]))
    go(cp(nblk(y, 0), nblk(y, 0), 9, sib))
    put(y, 0)
    finals = [
        pltpu.make_async_copy(masb, nm_out, lsem.at[1]),
        pltpu.make_async_copy(m1b, n1_out, lsem.at[2]),
        pltpu.make_async_copy(m2b, n2_out, lsem.at[3]),
    ]
    for c in finals:
        c.start()
    first, second = nblk(y, 1, 0), nblk(y, 1, 1)
    await_(first, 8)
    go(cp(first, first, 2, to_y[0]))
    for d in (0, 1):
        part = nblk(from_y[d], 0, d)
        await_(part, d)
        go(cp(part, part, 4 + d, to_y[d]))
    for d in (0, 1):
        await_(nblk(from_y[d], 0, 1 - d), 20 + d)
        b = nblk(from_y[d], 0)
        go(cp(b, b, 11 + d, sib))
        put(from_y[d], 0)
    await_(second, 17)
    go(cp(second, second, 3, to_y[1]))
    go(cp(second, second, 18, to_y[0]))
    go(cp(first, first, 19, to_y[1]))
    for t in range(4, 8):
        hgsend(t).start()
    b = nblk(y, 1)
    go(cp(b, b, 10, sib))
    put(y, 1)
    b = nblk(y2, 0)
    for d in (0, 1):
        await_(nblk(y2, 0, d), 4 + d)
    go(cp(b, b, 15, sib))
    put(y2, 0)
    for d in (0, 1):
        part = nblk(from_y[d], 1, d)
        await_(part, 2 + d)
        go(cp(part, part, 6 + d, to_y[d]))
    for d in (0, 1):
        await_(nblk(from_y[d], 1, 1 - d), 18 + d)
        b = nblk(from_y[d], 1)
        go(cp(b, b, 13 + d, sib))
        put(from_y[d], 1)
    oc = 1 - core

    def from_sibling(yy, j, i):
        await_(nblk(yy, j, cc=oc), i)
        put(yy, j, oc)

    from_sibling(y, 0, 9)
    from_sibling(y, 1, 10)
    from_sibling(yl1, 0, 11)
    from_sibling(yr1, 0, 12)
    from_sibling(y2, 0, 15)
    b = nblk(y2, 1)
    for d in (0, 1):
        await_(nblk(y2, 1, d), 6 + d)
    go(cp(b, b, 16, sib))
    put(y2, 1)
    from_sibling(yl1, 1, 13)
    from_sibling(yr1, 1, 14)
    from_sibling(y2, 1, 16)

    got(hts, g_r)
    got(hts, lsem.at[4])
    for c in finals:
        c.wait()
    got(nwb, w_s)
    got(hts, g_s)
    got(hts, hss)
    got(cbuf.at[pl.ds(0, 7)], zs)
    got(gs.at[0, 0, pl.ds(0, 336), :], wxs)
    got(gs.at[pl.ds(0, 3), 0], wys)
    got(gs.at[:, 0], wds)
    got(gs, ds_)
    got(yfs, yf_s)
    got(yns, yn_s)
    got(xs.at[pl.ds(0, 3)], x_s)
    got(nr, n_s)
    got(nwb.at[:, pl.ds(0, 3840)], o_s)


def local(hidden, cotangent, master, moment_one, moment_two):
    dma = pltpu.SemaphoreType.DMA
    any_ = pl.BlockSpec(memory_space=pl.ANY)
    v = pltpu.VMEM
    scratch = [
        v((NK, 1024, 512), BF16),
        v((2, 2, 2, 2, FC, 512), BF16),
        v((2, FC, 1024), BF16),
        v((FC, 1024), BF16),
        v((4, 2, FC, 512), F32),
        v((4, 2, FC, 512), F32),
        v((4, 2, FC, 128), BF16),
        v((4, 2, FC, 128), BF16),
        v((4, 2, 2, FC, 128), BF16),
        v((4, 2, 2, FC, 128), BF16),
        v((4, 2, FC, 128), BF16),
        v((2, 3, FC, 128), BF16),
        v((2, FC, 128), F32),
        v((2, FC, 1024), F32),
        v((2, FC, 1024), BF16),
        v((FC, 256), F32),
        v((FC, 256), F32),
        v((FC, 256), F32),
        v((FC, 4096), BF16),
        v((3, 1, 128), F32),
        v((17, 1, 128), F32),
        dma((5,)),
        dma((NK,)),
        dma, dma((NK, 4)),
        dma, dma,
        dma, dma((2,)),
        dma, dma((2,)),
        dma, dma,
        dma, dma((4, 2)),
        dma, dma((4, 2)),
        dma, dma((4,)),
        dma, dma,
        dma, dma,
        dma, dma((3,)),
        dma, dma((22,)),
        dma,
    ]
    sds = jax.ShapeDtypeStruct
    hg, nw, nm, n1, n2 = pl.pallas_call(
        kernel,
        out_shape=(
            sds((FC, 2048), BF16),
            sds((FC, 4096), BF16),
            sds((FC, 256), F32),
            sds((FC, 256), F32),
            sds((FC, 256), F32),
        ),
        in_specs=[any_] * 5,
        out_specs=(any_,) * 5,
        scratch_shapes=scratch,
        compiler_params=pltpu.CompilerParams(
            collective_id=0, has_side_effects=True, vmem_limit_bytes=63 * 2**20
        ),
        cost_estimate=pl.CostEstimate(
            flops=15_032_385_536, bytes_accessed=16_000_000, transcendentals=0
        ),
        name="fused_backward",
    )(hidden.T, cotangent, master.T, moment_one.T, moment_two.T)
    outs = (hg, nw, nm, n1, n2)
    hg, nw, nm, n1, n2 = pl.pallas_call(
        hand_on,
        out_shape=tuple(sds(t.shape, t.dtype) for t in outs),
        in_specs=[any_] * 5,
        out_specs=(any_,) * 5,
        scratch_shapes=[v(t.shape, t.dtype) for t in outs] + [dma((2, 11))],
        compiler_params=pltpu.CompilerParams(vmem_limit_bytes=60 * 2**20),
        name="hand_on",
    )(*outs)
    return (hg.T, nw.T, nm.T, n1.T, n2.T)


def hand_on(*refs):
    srcs, dsts, bufs, sems = refs[:5], refs[5:10], refs[10:15], refs[15]
    ins, outs = [], []
    for src, dst, buf in zip(srcs, dsts, bufs):
        n = 4 if src.shape[1] > 256 else 1
        rows = FC // n
        for i in range(n):
            cut = pl.ds(i * rows, rows)
            k = len(ins)
            ins.append(pltpu.make_async_copy(src.at[cut, :], buf.at[cut, :], sems.at[0, k]))
            outs.append(pltpu.make_async_copy(buf.at[cut, :], dst.at[cut, :], sems.at[1, k]))
    for c in ins:
        c.start()
    for c, d in zip(ins, outs):
        c.wait()
        d.start()
    for d in outs:
        d.wait()


def solution(mesh):
    return jax.shard_map(
        local,
        mesh=mesh,
        in_specs=(
            P("dp", "mp"),
            P(("dp", "mp"), None),
            P("dp", "mp"),
            P("dp", "mp"),
            P("dp", "mp"),
        ),
        out_specs=(P("dp", "mp"), P(None, "mp"), P("dp", "mp"), P("dp", "mp"), P("dp", "mp")),
        check_vma=False,
    )
```
